32 devices in a mesh: space: 16 (over z, y, core), vel: 2 (over x).
Axes of the slice: x: 2, y: 2, z: 4, core: 2. Of those that a mesh axis runs over, the one named last changes fastest.
Arguments:
- dist: float32 [13824, 8192], P('vel', 'space'), may hold values from 0.02 to 45, as said below
- free_stream: float32 [13824], P('vel'), may hold values from 0.36 to 14, as said below
- area_normal: float32 [18, 8192], P(None, 'space'), may hold values from -2.7 to 2.7
- cell_volume: float32 [8192], P('space'), may hold values from 0.5 to 2
- face_nbr: int32 [6, 8192], P(None, 'space'), may hold values from 0 to 1023
- face_type: int32 [6, 8192], P(None, 'space'), may hold values from 0 to 2, as said below
- send_list: int32 [4, 2048], P(None, 'space'), may hold values from 0 to 511
Outputs:
- dist_new: float32 [13824, 8192], P('vel', 'space')
The draws below stay inside these ranges and needn't reach their ends.
Inputs may be any that keep to these rules, and one draw needn't show every extreme that they name: `dist`: every entry is positive. `free_stream`: every entry is positive. `face_nbr`: an entry s at or above 512 names received slot s - 512; entries are read only where face_type is 0. `face_type`: 0 interior or partition face, 1 inflow, 2 outflow. `send_list`: local cell numbers of the sending partition.
All inputs are finite; a program needn't handle non-finite values.
Results may differ from the reference program's by a relative error of at most 0.0003.
Values sent between devices are 32-bit elements; how exact they have to be, the bound alone decides.
No kernel may reach another device: no remote copies, remote signals or barrier semaphores. Data moves between devices by JAX's collectives and lax.ppermute only.
A program may use at most 256 MiB of HBM per device.

```python
import math
import jax
import jax.numpy as jnp
from jax import lax

NODES = 24
VELS = 13824
CELL_DEV = 512
SEND = 128
DIRS = 4
FACES = 6
CELLS = 8192
N_SPACE = 16


def speed_axes():
    vel_index = jnp.arange(VELS, dtype=jnp.int32)
    half = (NODES - 1) / 2.0
    first = (vel_index // (NODES * NODES)).astype(jnp.float32)
    second = (vel_index // NODES % NODES).astype(jnp.float32)
    last_axis = (vel_index % NODES).astype(jnp.float32)
    return (first - half, second - half, last_axis - half)


def draw_dist(key, part):
    key = jax.random.fold_in(key, 11)
    cell_key, entry_key = jax.random.split(key)
    speed_x, speed_y, speed_z = speed_axes()
    cell_scale = jnp.exp(jax.random.uniform(cell_key, (CELLS,), jnp.float32, -0.7, 0.7))
    noise_part = jax.random.uniform(entry_key, (VELS, CELLS), jnp.float32, -1.0, 1.0)
    return cell_scale[None, :] * jnp.exp(0.1 * speed_x[:, None] + noise_part)


def draw_free_stream(key, part):
    key = jax.random.fold_in(key, 13)
    beam_key, floor_key = jax.random.split(key)
    speed_x, speed_y, speed_z = speed_axes()
    beam = 4.0 * jnp.exp(-((speed_x - 8.0) ** 2 + speed_y ** 2 + speed_z ** 2) / 4.0)
    beam_noise = jax.random.uniform(beam_key, (VELS,), jnp.float32, -1.0, 1.0)
    floor_noise = jax.random.uniform(floor_key, (VELS,), jnp.float32, -1.0, 1.0)
    return beam * jnp.exp(beam_noise) + jnp.exp(floor_noise)


def draw_area_normal(key, part):
    key = jax.random.fold_in(key, 12)
    scale_key, tilt_key = jax.random.split(key)
    face_scale = jnp.exp(jax.random.uniform(scale_key, (FACES, CELLS), jnp.float32, -0.7, 0.7))
    tilt = jax.random.uniform(tilt_key, (FACES, 3, CELLS), jnp.float32, -0.3, 0.3)
    face_ids = jnp.arange(FACES, dtype=jnp.int32)[:, None]
    dim_ids = jnp.arange(3, dtype=jnp.int32)[None, :]
    main_part = jnp.where(dim_ids == face_ids // 2, 1.0 - 2.0 * (face_ids % 2).astype(jnp.float32), 0.0)
    return (face_scale[:, None, :] * (main_part[:, :, None] + tilt)).reshape(3 * FACES, CELLS)


def draw_face_type(key, part):
    key = jax.random.fold_in(key, 14)
    picked = jax.random.randint(key, (FACES, CELLS), 0, 10, dtype=jnp.int32)
    return jnp.where(picked < 7, 0, jnp.where(picked < 9, 1, 2)).astype(jnp.int32)


def place_ends(values, rng, low, top_value):
    longest = values.shape.index(max(values.shape))
    spots = []
    for shift in (0, 1):
        where = [jax.random.randint(jax.random.fold_in(rng, axis), (), 0, length) for axis, length in enumerate(values.shape)]
        where[longest] = (where[longest] + shift) % values.shape[longest]
        spots.append(tuple(where))
    return values.at[spots[0]].set(low).at[spots[1]].set(top_value)


def block_scale(own_key, dims, cuts, smallest, largest):
    factor_of, own = 1.0, jax.random.fold_in(own_key, 6)
    for axis_at, blocks in cuts:
        heights = jnp.exp(jax.random.uniform(jax.random.fold_in(own, axis_at), (blocks,), jnp.float32, smallest / len(cuts), largest / len(cuts)))
        factor_of = factor_of * jnp.repeat(heights, dims[axis_at] // blocks).reshape([-1 if axis == axis_at else 1 for axis in range(len(dims))])
    return factor_of


def setup_inputs(seed: int = 0) -> dict:
    keys = jax.random.split(jax.random.key(seed), 8)
    dist = draw_dist(jax.random.fold_in(keys[7], 71), 0)
    free_stream = draw_free_stream(jax.random.fold_in(keys[7], 71), 0)
    area_normal = draw_area_normal(jax.random.fold_in(keys[7], 71), 0)
    cell_volume = jnp.clip(jnp.exp(math.log(2.0) - 1.3862944 * jax.random.uniform(keys[3], (CELLS,), jnp.float32) ** block_scale(keys[3], (CELLS,), ((0, 16),), -0.2, 0.2)), 0.5, 2.0)
    face_nbr = place_ends(jax.random.randint(keys[4], (FACES, CELLS), 0, CELL_DEV + DIRS * SEND), jax.random.fold_in(keys[4], 1), 0, (CELL_DEV + DIRS * SEND) - 1).astype(jnp.int32)
    face_type = draw_face_type(jax.random.fold_in(keys[7], 71), 0)
    send_list = place_ends(jax.random.randint(keys[6], (DIRS, SEND * N_SPACE), 0, CELL_DEV), jax.random.fold_in(keys[6], 1), 0, CELL_DEV - 1).astype(jnp.int32)
    return {"dist": dist, "free_stream": free_stream, "area_normal": area_normal, "cell_volume": cell_volume, "face_nbr": face_nbr, "face_type": face_type, "send_list": send_list}


CFL = 0.9
MU_REF = 60.0
OMEGA = 0.81
PRANDTL = 2.0 / 3.0
neighbour_steps = (1, -1, 2, -2)

def grid_speeds(vel_index):
    spacing = 24.0 / NODES
    half = (NODES - 1) / 2.0
    first = (vel_index // (NODES * NODES)).astype(jnp.float32)
    second = (vel_index // NODES % NODES).astype(jnp.float32)
    last_axis = (vel_index % NODES).astype(jnp.float32)
    return ((first - half) * spacing, (second - half) * spacing, (last_axis - half) * spacing)

def source_columns(face_nbr, send_list):
    partition = (jnp.arange(CELLS, dtype=jnp.int32) // CELL_DEV)[None, :]
    local_face = face_nbr < CELL_DEV
    received = jnp.maximum(face_nbr - CELL_DEV, 0)
    direction = received // SEND
    within = received % SEND
    steps_table = jnp.array(neighbour_steps, dtype=jnp.int32)
    source_part = (partition - steps_table[direction]) % N_SPACE
    remote_cell = send_list[direction, source_part * SEND + within]
    return jnp.where(local_face, partition * CELL_DEV + face_nbr, source_part * CELL_DEV + remote_cell).astype(jnp.int32)

def hydrodynamic_variables(integral_averages):
    specific_matter_amount = integral_averages[0]
    mean_gas_speed = [integral_averages[1 + axis] / specific_matter_amount for axis in range(3)]
    particle_contribution = mean_gas_speed[0] ** 2 + mean_gas_speed[1] ** 2 + mean_gas_speed[2] ** 2
    local_thermal_level = (2.0 * integral_averages[4] / specific_matter_amount - particle_contribution) / 3.0
    return (specific_matter_amount, mean_gas_speed, local_thermal_level)

def reference(dist, free_stream, area_normal, cell_volume, face_nbr, face_type, send_list):
    speeds = grid_speeds(jnp.arange(VELS, dtype=jnp.int32))
    spacing = 24.0 / NODES
    weight = spacing ** 3
    top_speed = (NODES - 1) / 2.0 * spacing * math.sqrt(3.0)
    normals = area_normal.reshape(FACES, 3, CELLS)
    face_areas = jnp.sqrt(lax.optimization_barrier(jnp.sum(normals * normals, axis=1)))
    cell_limit = cell_volume / (top_speed * lax.optimization_barrier(jnp.sum(face_areas, axis=0)))
    time_step = CFL * jnp.min(cell_limit)
    step_ratio = time_step / cell_volume
    sources = source_columns(face_nbr, send_list)
    columns = [speeds[axis][:, None] for axis in range(3)]
    speed_sq = columns[0] ** 2 + columns[1] ** 2 + columns[2] ** 2

    def moments_of(field):
        return jnp.stack([weight * lax.optimization_barrier(jnp.sum(field, axis=0)), weight * lax.optimization_barrier(jnp.sum(columns[0] * field, axis=0)), weight * lax.optimization_barrier(jnp.sum(columns[1] * field, axis=0)), weight * lax.optimization_barrier(jnp.sum(columns[2] * field, axis=0)), weight * lax.optimization_barrier(jnp.sum(0.5 * speed_sq * field, axis=0))])

    def one_part(partition_id):
        start = partition_id * CELL_DEV
        own_cells = lax.dynamic_slice_in_dim(dist, start, CELL_DEV, 1)
        block_sources = lax.dynamic_slice_in_dim(sources, start, CELL_DEV, 1)
        block_normals = lax.dynamic_slice_in_dim(normals, start, CELL_DEV, 2)
        block_kinds = lax.dynamic_slice_in_dim(face_type, start, CELL_DEV, 1)
        block_ratio = lax.dynamic_slice_in_dim(step_ratio, start, CELL_DEV, 0)
        flux_total = jnp.zeros_like(own_cells)
        for face_slot in range(FACES):
            normal_speed = columns[0] * block_normals[face_slot, 0] + columns[1] * block_normals[face_slot, 1] + columns[2] * block_normals[face_slot, 2]
            outside = jnp.take(dist, block_sources[face_slot], axis=1)
            face_kind = block_kinds[face_slot]
            outside = jnp.where(face_kind == 0, outside, jnp.where(face_kind == 1, free_stream[:, None], own_cells))
            flux_total = flux_total + jnp.where(normal_speed > 0, normal_speed * own_cells, normal_speed * outside)
        invariant_quantities = moments_of(own_cells)
        specific_matter_amount, mean_gas_speed, local_thermal_level = hydrodynamic_variables(invariant_quantities)
        rel_old = [columns[axis] - mean_gas_speed[axis] for axis in range(3)]
        rel_old_sq = rel_old[0] ** 2 + rel_old[1] ** 2 + rel_old[2] ** 2
        heat_flux = [0.5 * weight * lax.optimization_barrier(jnp.sum(rel_old[axis] * rel_old_sq * own_cells, axis=0)) for axis in range(3)]
        new_moments = invariant_quantities - block_ratio[None, :] * moments_of(flux_total)
        density_new, mean_new, temp_new = hydrodynamic_variables(new_moments)
        relax_time = MU_REF * temp_new ** OMEGA / (density_new * temp_new)
        relax_ratio = time_step / relax_time
        rel_new = [columns[axis] - mean_new[axis] for axis in range(3)]
        rel_sq = rel_new[0] ** 2 + rel_new[1] ** 2 + rel_new[2] ** 2
        maxwell = density_new * (2.0 * math.pi * temp_new) ** (-1.5) * jnp.exp(-rel_sq / (2.0 * temp_new))
        along_heat = rel_new[0] * heat_flux[0] + rel_new[1] * heat_flux[1] + rel_new[2] * heat_flux[2]
        shakhov = maxwell * (1.0 + (1.0 - PRANDTL) * along_heat / (5.0 * density_new * temp_new * temp_new) * (rel_sq / temp_new - 5.0))
        transported = own_cells - block_ratio[None, :] * flux_total
        return (transported + relax_ratio * shakhov) / (1.0 + relax_ratio)
    blocks = lax.map(one_part, jnp.arange(N_SPACE, dtype=jnp.int32))
    return jnp.moveaxis(blocks, 0, 1).reshape(VELS, CELLS)
```

```python
import functools
import math

import jax
import jax.numpy as jnp
from jax import lax
from jax.experimental import pallas as pl
from jax.experimental.pallas import tpu as pltpu
from jax.sharding import PartitionSpec as P

NODES = 24
PLANE = NODES * NODES
HALF = (NODES - 1) / 2.0
FACES = 6
CFL = 0.9
MU_REF = 60.0
OMEGA = 0.81
PRANDTL = 2.0 / 3.0
neighbour_steps = (1, -1, 2, -2)

LANES = 128
SUB = 8
F32 = jnp.float32
BF16 = jnp.bfloat16
VMEM_LIMIT = 56 * 1024 * 1024


def passed_along(block, axis, distance):
    count = lax.axis_size(axis)
    route = [((i - distance) % count, i) for i in range(count)]
    return lax.ppermute(block, axis, route)


def chunk_plan(planes):
    if planes < 3:
        return [1] * planes
    rounds = max(1, -(-(planes - 2) // 3))
    inner = [(planes - 2) // rounds + (i < (planes - 2) % rounds) for i in range(rounds)]
    return [1] + inner + [1]


def put_split(src_ref, split_ref, at, step=48):
    rows, width = src_ref.shape
    full = split_ref.shape[1] // 2

    @pl.loop(0, rows // step)
    def _(i):
        here = pl.ds(pl.multiple_of(i * step, 16), step)
        value = src_ref[here, :]
        upper = value.astype(BF16)
        split_ref[here, at : at + width] = upper
        split_ref[here, full + at : full + at + width] = (value - upper.astype(F32)).astype(BF16)


def put_one_hot(pick_ref, at, row, step=64):
    height, width = pick_ref.shape[0], row.shape[1]

    @pl.loop(0, height // step)
    def _(i):
        first = pl.multiple_of(i * step, 16)
        index = lax.broadcasted_iota(jnp.int32, (step, width), 0) + first
        pick_ref[pl.ds(first, step), at : at + width] = jnp.where(index == row, 1.0, 0.0).astype(BF16)


def picked(split, pick):
    return jnp.dot(split, jnp.concatenate([pick, pick], axis=0), preferred_element_type=F32)


def send_kernel(dist_ref, send_ref, *refs):
    outs, (split_ref, pick_ref) = refs[:-2], refs[-2:]
    width = send_ref.shape[1]

    @pl.when(pl.program_id(0) == 0)
    def _():
        for o in range(len(outs)):
            put_one_hot(pick_ref, o * width, send_ref[o : o + 1, :])

    put_split(dist_ref, split_ref, 0)
    out = picked(split_ref[...], pick_ref[...])
    for o, out_ref in enumerate(outs):
        out_ref[...] = out[:, o * width : (o + 1) * width]


def rows8(row):
    return jnp.broadcast_to(row, (SUB, row.shape[-1]))


def put_normals(normal_ref, x_ref, y_ref, z_ref):
    cells = normal_ref.shape[1]
    last = lax.broadcasted_iota(jnp.int32, (NODES, cells), 0).astype(F32) - HALF
    total = [jnp.zeros((1, cells), F32)] * 3
    for k in range(FACES + 1):
        parts = [normal_ref[3 * k + a : 3 * k + a + 1, :] for a in range(3)] if k < FACES else total
        if k < FACES:
            total = [total[a] + parts[a] for a in range(3)]
        x_ref[k * SUB : (k + 1) * SUB, :] = rows8(parts[0])
        y_ref[k * SUB : (k + 1) * SUB, :] = rows8(parts[1])
        z_ref[k * NODES : (k + 1) * NODES, :] = last * parts[2]


def last_speeds():
    index = lax.broadcasted_iota(jnp.int32, (SUB, LANES), 0).astype(F32) - HALF
    return [index + float(j * SUB) for j in range(NODES // SUB)]


def z_sums(tiles, speeds, powers):
    sums, terms = [], list(tiles)
    for p in range(powers):
        if p:
            terms = [t * c for t, c in zip(terms, speeds)]
        sums.append(terms[0] + terms[1] + terms[2])
    return sums


def rest_of_moments(sums, first):
    energy = 0.5 * (first * first * sums[0, 0] + sums[0, 1 + 1] + sums[2, 0])
    return [sums[0, 0], first * sums[0, 0], sums[0, 1], sums[1, 0], energy]


def add_rows(acc_ref, values, lanes):
    for m, value in enumerate(values):
        acc_ref[m * SUB : (m + 1) * SUB, lanes] += value


def sum_rows(acc_ref, count):
    return [jnp.sum(acc_ref[m * SUB : (m + 1) * SUB, :], axis=0, keepdims=True) for m in range(count)]


FLUX_KEYS = ((0, 0), (0, 1), (0, 2), (1, 0), (2, 0))
DIST_KEYS = ((0, 0), (0, 1), (0, 2), (0, 3), (1, 0), (1, 1), (1, 2), (2, 0), (2, 1), (3, 0))


def grow(carry, keys, sums, second):
    powers = [None, second, second * second, second * second * second]
    return tuple(
        c + (sums[i] if j == 0 else sums[i] * powers[j]) for c, (i, j) in zip(carry, keys)
    )


def near_kernel(
    plane_ref, dist_ref, stream_ref, normal_ref, nbr_ref, kind_ref, after_ref,
    flux_ref, dist_sum_ref, flux_sum_ref, far_ref,
    split_ref, pick_ref, out_ref, x_ref, y_ref, z_ref, inflow_ref, dist_acc, flux_acc,
):
    step = pl.program_id(0)
    cells = dist_ref.shape[1]

    @pl.when(step == 0)
    def _():
        own = lax.broadcasted_iota(jnp.int32, (1, cells), 1)
        for k in range(FACES):
            nbr, kind = nbr_ref[k : k + 1, :], kind_ref[k : k + 1, :]
            near = jnp.where((kind == 0) & (nbr < cells), nbr, jnp.where(kind == 2, own, -1))
            far = jnp.where((kind == 0) & (nbr >= cells), nbr - cells, -1)
            put_one_hot(pick_ref, k * cells, near)
            put_one_hot(far_ref, k * cells, far)
            inflow_ref[k * SUB : (k + 1) * SUB, :] = rows8(jnp.where(kind == 1, 1.0, 0.0))
        put_normals(normal_ref, x_ref, y_ref, z_ref)
        dist_acc[...] = jnp.zeros_like(dist_acc)
        flux_acc[...] = jnp.zeros_like(flux_acc)

    put_split(dist_ref, split_ref, 0)
    for k in range(FACES):
        out_ref[k] = picked(split_ref[...], pick_ref[:, k * cells : (k + 1) * cells])
    first = (plane_ref[0] + step).astype(F32) - HALF
    speeds = last_speeds()
    tiles = range(NODES // SUB)
    for t in range(cells // LANES):
        lanes = slice(t * LANES, (t + 1) * LANES)
        base_x = [x_ref[k * SUB : (k + 1) * SUB, lanes] * first for k in range(FACES + 1)]

        def body(y, carry, lanes=lanes, base_x=base_x):
            second = y.astype(F32) - HALF
            rows = [pl.ds(pl.multiple_of(y * NODES + j * SUB, SUB), SUB) for j in tiles]
            own = [dist_ref[r, lanes] for r in rows]
            stream = [stream_ref[r, :] for r in rows]
            acc, low = [0.0 for _ in tiles], [0.0 for _ in tiles]
            for k in range(FACES):
                base = base_x[k] + y_ref[k * SUB : (k + 1) * SUB, lanes] * second
                inflow = inflow_ref[k * SUB : (k + 1) * SUB, lanes] > 0.5
                for j in tiles:
                    z = z_ref[k * NODES + j * SUB : k * NODES + (j + 1) * SUB, lanes]
                    inward = jnp.minimum(base + z, 0.0)
                    outside = jnp.where(inflow, stream[j], out_ref[k, rows[j], lanes])
                    acc[j] += inward * outside
                    low[j] += inward
            k = FACES
            base = base_x[k] + y_ref[k * SUB : (k + 1) * SUB, lanes] * second
            flux = []
            for j in tiles:
                z = z_ref[k * NODES + j * SUB : k * NODES + (j + 1) * SUB, lanes]
                flux.append(acc[j] + (base + z - low[j]) * own[j])
                flux_ref[rows[j], lanes] = flux[j]
            dist_part = grow(carry[0], DIST_KEYS, z_sums(own, speeds, 4), second)
            flux_part = grow(carry[1], FLUX_KEYS, z_sums(flux, speeds, 3), second)
            return dist_part, flux_part

        zero = jnp.zeros((SUB, LANES), F32)
        dist_part, flux_part = lax.fori_loop(
            0, NODES, body, ((zero,) * len(DIST_KEYS), (zero,) * len(FLUX_KEYS))
        )
        s = dict(zip(DIST_KEYS, dist_part))
        square = first * first
        add_rows(
            dist_acc,
            rest_of_moments(s, first)
            + [
                square * s[0, 0], s[0, 2], s[2, 0],
                first * s[0, 1], first * s[1, 0], s[1, 1],
                first * (square * s[0, 0] + s[0, 2] + s[2, 0]),
                square * s[0, 1] + s[0, 3] + s[2, 1],
                square * s[1, 0] + s[1, 2] + s[3, 0],
            ],
            lanes,
        )
        add_rows(flux_acc, rest_of_moments(dict(zip(FLUX_KEYS, flux_part)), first), lanes)

    @pl.when(step == pl.num_programs(0) - 1)
    def _():
        dist_sum_ref[...] = jnp.concatenate(
            sum_rows(dist_acc, 14) + [jnp.zeros((2, cells), F32)], axis=0
        )
        flux_sum_ref[...] = jnp.concatenate(
            sum_rows(flux_acc, 5) + [jnp.zeros((3, cells), F32)], axis=0
        )


def far_kernel(
    sends, plane_ref, time_ref, dist_ref, flux_ref, far_ref, normal_ref, volume_ref, before_ref, *refs
):
    arrived, refs = refs[:sends], refs[sends:]
    moved_ref, flux_sum_ref, split_ref, out_ref, x_ref, y_ref, z_ref, flux_acc, ratio_ref = refs
    step = pl.program_id(0)
    cells = dist_ref.shape[1]

    @pl.when(step == 0)
    def _():
        put_normals(normal_ref, x_ref, y_ref, z_ref)
        flux_acc[...] = jnp.zeros_like(flux_acc)
        ratio_ref[...] = rows8(time_ref[0, 0] / volume_ref[...])

    for o, block_ref in enumerate(arrived):
        put_split(block_ref, split_ref, o * block_ref.shape[1])
    for k in range(FACES):
        out_ref[k] = picked(split_ref[...], far_ref[:, k * cells : (k + 1) * cells])
    first = (plane_ref[0] + step).astype(F32) - HALF
    speeds = last_speeds()
    tiles = range(NODES // SUB)
    for t in range(cells // LANES):
        lanes = slice(t * LANES, (t + 1) * LANES)
        base_x = [x_ref[k * SUB : (k + 1) * SUB, lanes] * first for k in range(FACES)]
        ratio = ratio_ref[:, lanes]

        def body(y, carry, lanes=lanes, base_x=base_x, ratio=ratio):
            second = y.astype(F32) - HALF
            rows = [pl.ds(pl.multiple_of(y * NODES + j * SUB, SUB), SUB) for j in tiles]
            acc = [0.0 for _ in tiles]
            for k in range(FACES):
                base = base_x[k] + y_ref[k * SUB : (k + 1) * SUB, lanes] * second
                for j in tiles:
                    z = z_ref[k * NODES + j * SUB : k * NODES + (j + 1) * SUB, lanes]
                    acc[j] += jnp.minimum(base + z, 0.0) * out_ref[k, rows[j], lanes]
            for j in tiles:
                moved_ref[rows[j], lanes] = dist_ref[rows[j], lanes] - ratio * (
                    flux_ref[rows[j], lanes] + acc[j]
                )
            return grow(carry, FLUX_KEYS, z_sums(acc, speeds, 3), second)

        zero = jnp.zeros((SUB, LANES), F32)
        part = lax.fori_loop(0, NODES, body, (zero,) * len(FLUX_KEYS))
        add_rows(flux_acc, rest_of_moments(dict(zip(FLUX_KEYS, part)), first), lanes)

    @pl.when(step == pl.num_programs(0) - 1)
    def _():
        flux_sum_ref[...] = before_ref[...] + jnp.concatenate(
            sum_rows(flux_acc, 5) + [jnp.zeros((3, cells), F32)], axis=0
        )


def hydrodynamic_variables(moments):
    density = moments[0]
    mean = [moments[1 + axis] / density for axis in range(3)]
    square = mean[0] ** 2 + mean[1] ** 2 + mean[2] ** 2
    return density, mean, (2.0 * moments[4] / density - square) / 3.0


def relax_kernel(
    plane_ref, time_ref, moved_ref, dist_sum_ref, flux_sum_ref, volume_ref, out_ref,
    x_ref, y_ref, z_ref, cell_ref,
):
    step = pl.program_id(0)
    cells = moved_ref.shape[1]

    @pl.when(step == 0)
    def _():
        time_step = time_ref[0, 0]
        ratio = time_step / volume_ref[...]
        sums = [dist_sum_ref[m : m + 1, :] for m in range(14)]
        density, mean, _ = hydrodynamic_variables(sums)
        xx, yy, zz, xy, xz, yz = sums[5:11]
        pairs = ((xx, xy, xz), (xy, yy, yz), (xz, yz, zz))
        square = mean[0] ** 2 + mean[1] ** 2 + mean[2] ** 2
        heat = []
        for a in range(3):
            cross = mean[0] * pairs[a][0] + mean[1] * pairs[a][1] + mean[2] * pairs[a][2]
            heat.append(
                0.5
                * (
                    sums[11 + a] - mean[a] * (2.0 * sums[4]) - 2.0 * cross
                    + 2.0 * mean[a] * square * density
                )
            )
        new = [sums[m] - ratio * flux_sum_ref[m : m + 1, :] for m in range(5)]
        density, mean, temp = hydrodynamic_variables(new)
        relax_time = MU_REF * jnp.exp(OMEGA * jnp.log(temp)) / (density * temp)
        relax = time_step / relax_time
        keep = 1.0 / (1.0 + relax)
        root = lax.rsqrt(2.0 * math.pi * temp)
        front = relax * keep * density * root * root * root
        along = (1.0 - PRANDTL) / (5.0 * density * temp * temp)
        for m, row in enumerate((keep, mean[0], temp, heat[0] * along, front)):
            cell_ref[m * SUB : (m + 1) * SUB, :] = rows8(row)
        nodes = lax.broadcasted_iota(jnp.int32, (NODES, cells), 0).astype(F32) - HALF
        for a, ref in ((1, y_ref), (2, z_ref)):
            rel = nodes - mean[a]
            square = rel * rel / temp
            for i, table in enumerate((jnp.exp(-0.5 * square), square, rel * heat[a] * along)):
                if a == 2:
                    ref[i * NODES : (i + 1) * NODES, :] = table
                    continue
                for y in range(NODES):
                    ref[i, y] = rows8(table[y : y + 1, :])

    keep, mean, temp, heat, front = [
        cell_ref[m * SUB : (m + 1) * SUB, :] for m in range(5)
    ]
    rel = (plane_ref[0] + step).astype(F32) - HALF - mean
    square = rel * rel / temp
    x_ref[0] = front * jnp.exp(-0.5 * square)
    x_ref[1] = square - 5.0
    x_ref[2] = rel * heat
    tiles = range(NODES // SUB)
    for t in range(cells // LANES):
        lanes = slice(t * LANES, (t + 1) * LANES)
        from_x = [x_ref[i, :, lanes] for i in range(3)]
        keep = cell_ref[0:SUB, lanes]

        @pl.loop(0, NODES)
        def _(y, lanes=lanes, from_x=from_x, keep=keep):
            from_y = [y_ref[i, y, :, lanes] for i in range(3)]
            peak = from_x[0] * from_y[0]
            square = from_x[1] + from_y[1]
            along = from_x[2] + from_y[2]
            for j in tiles:
                row = pl.ds(pl.multiple_of(y * NODES + j * SUB, SUB), SUB)
                z = [z_ref[i * NODES + j * SUB : i * NODES + (j + 1) * SUB, lanes] for i in range(3)]
                shape = (along + z[2]) * (square + z[1]) + 1.0
                out_ref[row, lanes] = moved_ref[row, lanes] * keep + peak * z[0] * shape


def params():
    return pltpu.CompilerParams(
        vmem_limit_bytes=VMEM_LIMIT, dimension_semantics=("arbitrary",)
    )


def whole(*shape):
    return pl.BlockSpec(shape, lambda i: (0,) * len(shape))


def planes_from(first, width):
    return pl.BlockSpec((PLANE, width), lambda i: (first + i, 0))


SMEM = pl.BlockSpec(memory_space=pltpu.SMEM)


def gather_sends(dist, send_list, first, planes):
    cells, (dirs, width) = dist.shape[1], send_list.shape
    rows = planes * PLANE
    return pl.pallas_call(
        send_kernel,
        grid=(planes,),
        in_specs=[planes_from(first, cells), whole(dirs, width)],
        out_specs=[planes_from(0, width)] * dirs,
        out_shape=[jax.ShapeDtypeStruct((rows, width), F32)] * dirs,
        scratch_shapes=[
            pltpu.VMEM((PLANE, 2 * cells), BF16),
            pltpu.VMEM((cells, dirs * width), BF16),
        ],
        compiler_params=params(),
        cost_estimate=pl.CostEstimate(
            flops=rows * 4 * cells * dirs * width,
            bytes_accessed=4 * rows * (cells + dirs * width),
            transcendentals=0,
        ),
        name="listed_cells",
    )(dist, send_list)


def near_faces(plane, dist, stream, normals, face_nbr, face_type, slots, after):
    rows, cells = dist.shape
    planes = rows // PLANE
    return pl.pallas_call(
        near_kernel,
        grid=(planes,),
        in_specs=[
            SMEM, planes_from(0, cells), planes_from(0, LANES),
            whole(3 * FACES, cells), whole(FACES, cells), whole(FACES, cells),
            pl.BlockSpec(memory_space=pl.ANY),
        ],
        out_specs=[
            planes_from(0, cells), whole(16, cells), whole(8, cells), whole(slots, FACES * cells),
        ],
        out_shape=[
            jax.ShapeDtypeStruct((rows, cells), F32),
            jax.ShapeDtypeStruct((16, cells), F32),
            jax.ShapeDtypeStruct((8, cells), F32),
            jax.ShapeDtypeStruct((slots, FACES * cells), BF16),
        ],
        scratch_shapes=[
            pltpu.VMEM((PLANE, 2 * cells), BF16),
            pltpu.VMEM((cells, FACES * cells), BF16),
            pltpu.VMEM((FACES, PLANE, cells), F32),
            pltpu.VMEM(((FACES + 1) * SUB, cells), F32),
            pltpu.VMEM(((FACES + 1) * SUB, cells), F32),
            pltpu.VMEM(((FACES + 1) * NODES, cells), F32),
            pltpu.VMEM((FACES * SUB, cells), F32),
            pltpu.VMEM((14 * SUB, cells), F32),
            pltpu.VMEM((5 * SUB, cells), F32),
        ],
        compiler_params=params(),
        cost_estimate=pl.CostEstimate(
            flops=rows * 4 * cells * FACES * cells + 80 * rows * cells,
            bytes_accessed=4 * rows * 2 * cells,
            transcendentals=0,
        ),
        name="near_faces",
    )(plane, dist, stream, normals, face_nbr, face_type, after)


def far_faces(plane, time_step, dist, flux, pick, normals, volume, before, arrived, first, planes):
    cells = dist.shape[1]
    rows = planes * PLANE
    slots = pick.shape[0]
    return pl.pallas_call(
        functools.partial(far_kernel, len(arrived)),
        grid=(planes,),
        in_specs=[
            SMEM, SMEM, planes_from(first, cells), planes_from(first, cells),
            whole(slots, FACES * cells), whole(3 * FACES, cells), whole(1, cells), whole(8, cells),
        ]
        + [planes_from(0, block.shape[1]) for block in arrived],
        out_specs=[planes_from(first, cells), whole(8, cells)],
        out_shape=[
            jax.ShapeDtypeStruct(flux.shape, F32),
            jax.ShapeDtypeStruct((8, cells), F32),
        ],
        scratch_shapes=[
            pltpu.VMEM((PLANE, 2 * slots), BF16),
            pltpu.VMEM((FACES, PLANE, cells), F32),
            pltpu.VMEM(((FACES + 1) * SUB, cells), F32),
            pltpu.VMEM(((FACES + 1) * SUB, cells), F32),
            pltpu.VMEM(((FACES + 1) * NODES, cells), F32),
            pltpu.VMEM((5 * SUB, cells), F32),
            pltpu.VMEM((SUB, cells), F32),
        ],
        input_output_aliases={3: 0},
        compiler_params=params(),
        cost_estimate=pl.CostEstimate(
            flops=rows * 4 * slots * FACES * cells + 40 * rows * cells,
            bytes_accessed=4 * rows * (3 * cells + slots),
            transcendentals=0,
        ),
        name="far_faces",
    )(plane + first, time_step, dist, flux, pick, normals, volume, before, *arrived)


def relaxed(plane, time_step, moved, dist_sum, flux_sum, volume):
    rows, cells = moved.shape
    return pl.pallas_call(
        relax_kernel,
        grid=(rows // PLANE,),
        in_specs=[
            SMEM, SMEM, planes_from(0, cells), whole(16, cells), whole(8, cells), whole(1, cells),
        ],
        out_specs=planes_from(0, cells),
        out_shape=jax.ShapeDtypeStruct((rows, cells), F32),
        scratch_shapes=[
            pltpu.VMEM((3, SUB, cells), F32),
            pltpu.VMEM((3, NODES, SUB, cells), F32),
            pltpu.VMEM((3 * NODES, cells), F32),
            pltpu.VMEM((5 * SUB, cells), F32),
        ],
        compiler_params=params(),
        cost_estimate=pl.CostEstimate(
            flops=10 * rows * cells, bytes_accessed=8 * rows * cells, transcendentals=0
        ),
        name="relaxed",
    )(plane, time_step, moved, dist_sum, flux_sum, volume)


def least_over(value, axis):
    shift = 1
    while shift < lax.axis_size(axis):
        value = jnp.minimum(value, passed_along(value, axis, shift))
        shift *= 2
    return value


def local(dist, free_stream, area_normal, cell_volume, face_nbr, face_type, send_list):
    rows, cells = dist.shape
    planes = rows // PLANE
    dirs, width = send_list.shape
    plane = (lax.axis_index("vel") * planes).astype(jnp.int32).reshape(1)
    top_speed = HALF * math.sqrt(3.0)
    normals = area_normal.reshape(FACES, 3, cells)
    face_areas = jnp.sqrt(jnp.sum(normals * normals, axis=1))
    cell_limit = cell_volume / (top_speed * jnp.sum(face_areas, axis=0))
    time_step = CFL * least_over(jnp.min(cell_limit).reshape(1, 1), "space")
    volume = cell_volume.reshape(1, cells)

    arrived, first = [], 0
    for count in chunk_plan(planes):
        blocks = gather_sends(dist, send_list, first, count)
        moved = [
            passed_along(block, "space", distance)
            for block, distance in zip(blocks, neighbour_steps)
        ]
        arrived.append((first, count, moved))
        first += count
    stream = jnp.broadcast_to(free_stream[:, None], (rows, LANES))
    flux, dist_sum, flux_sum, pick = near_faces(
        plane, dist, stream, area_normal, face_nbr, face_type, dirs * width, blocks[-1]
    )
    dist_sum = lax.psum(dist_sum, "vel")
    for first, count, blocks in arrived:
        flux, flux_sum = far_faces(
            plane, time_step, dist, flux, pick, area_normal, volume, flux_sum, blocks, first, count
        )
    flux_sum = lax.psum(flux_sum, "vel")
    return relaxed(plane, time_step, flux, dist_sum, flux_sum, volume)


def solution(mesh):
    return jax.shard_map(
        local,
        mesh=mesh,
        in_specs=(
            P("vel", "space"),
            P("vel"),
            P(None, "space"),
            P("space"),
            P(None, "space"),
            P(None, "space"),
            P(None, "space"),
        ),
        out_specs=P("vel", "space"),
        check_vma=False,
    )
```

```python
import functools
import math

import jax
import jax.numpy as jnp
from jax import lax
from jax.experimental import pallas as pl
from jax.experimental.pallas import tpu as pltpu
from jax.sharding import PartitionSpec as P

NODES = 24
PLANE = NODES * NODES
HALF = (NODES - 1) / 2.0
FACES = 6
CFL = 0.9
MU_REF = 60.0
OMEGA = 0.81
PRANDTL = 2.0 / 3.0
neighbour_steps = (1, -1, 2, -2)

LANES = 128
SUB = 8
F32 = jnp.float32
VMEM_LIMIT = 60 * 1024 * 1024


def passed_along(block, axis, distance):
    count = lax.axis_size(axis)
    route = [((i - distance) % count, i) for i in range(count)]
    return lax.ppermute(block, axis, route)


def swapped(block, axis, start):
    count = lax.axis_size(axis)
    route = []
    for i in range(start, start + count, 2):
        route += [(i % count, (i + 1) % count), ((i + 1) % count, i % count)]
    return lax.ppermute(block, axis, route)


def summed_over(value, axis):
    count = lax.axis_size(axis)
    if count & (count - 1):
        return lax.psum(value, axis)
    reach = 1
    while reach < count:
        value = value + lax.ppermute(value, axis, [(i, i ^ reach) for i in range(count)])
        reach *= 2
    return value


def tiles_of(rows, i):
    return min(SUB, -(-rows // LANES) - i * SUB)


def turn(dist_ref, turned_ref):
    cells = dist_ref.shape[1]
    for s in range(SUB):
        for t in range(cells // LANES):
            block = dist_ref[s * LANES : (s + 1) * LANES, t * LANES : (t + 1) * LANES]
            turned_ref[pl.ds(t * LANES * SUB + s, LANES, stride=SUB), :] = block.T


def pick_rows(list_ref, row, turned_ref, picked_ref, out_ref):
    width = out_ref.shape[1]

    @pl.loop(0, width, unroll=8)
    def _(j):
        source = pl.ds(pl.multiple_of(list_ref[row, j] * SUB, SUB), SUB)
        picked_ref[pl.ds(pl.multiple_of(j * SUB, SUB), SUB), :] = turned_ref[source, :]

    for s in range(out_ref.shape[0]):
        out_ref[s] = picked_ref[pl.ds(s, width, stride=SUB), :]


def pick_lists(place_ref, list_ref, turned_ref, picked_ref, cross_ref, ahead_ref, back_ref):
    pick_rows(list_ref, 1 - place_ref[1], turned_ref, picked_ref, cross_ref)
    pick_rows(list_ref, 2, turned_ref, picked_ref, ahead_ref)
    pick_rows(list_ref, 3, turned_ref, picked_ref, back_ref)


def first_send_kernel(place_ref, list_ref, dist_ref, cross_ref, ahead_ref, back_ref, turned_ref, picked_ref):
    turn(dist_ref, turned_ref)
    pick_lists(place_ref, list_ref, turned_ref, picked_ref, cross_ref, ahead_ref, back_ref)


def send_kernel(place_ref, list_ref, turned_ref, after_ref, cross_ref, ahead_ref, back_ref, picked_ref):
    pick_lists(place_ref, list_ref, turned_ref.at[0], picked_ref, cross_ref, ahead_ref, back_ref)


def turn_kernel(place_ref, list_ref, dist_ref, after_ref, turned_ref, pair_ref, picked_ref):
    turn(dist_ref, turned_ref.at[0])
    pick_rows(list_ref, place_ref[1], turned_ref.at[0], picked_ref, pair_ref)


def rows8(row):
    return jnp.broadcast_to(row, (SUB, row.shape[-1]))


def last_speeds():
    index = lax.broadcasted_iota(jnp.int32, (SUB, LANES), 0).astype(F32) - HALF
    return [index + float(j * SUB) for j in range(NODES // SUB)]


def z_sums(tiles, speeds, powers):
    sums, terms = [], list(tiles)
    for p in range(powers):
        if p:
            terms = [t * c for t, c in zip(terms, speeds)]
        sums.append(terms[0] + terms[1] + terms[2])
    return sums


def rest_of_moments(sums, first):
    energy = 0.5 * (first * first * sums[0, 0] + sums[0, 1 + 1] + sums[2, 0])
    return [sums[0, 0], first * sums[0, 0], sums[0, 1], sums[1, 0], energy]


def add_rows(acc_ref, values, lanes):
    for m, value in enumerate(values):
        acc_ref[m * SUB : (m + 1) * SUB, lanes] += value


def sum_rows(acc_ref, count):
    return [jnp.sum(acc_ref[m * SUB : (m + 1) * SUB, :], axis=0, keepdims=True) for m in range(count)]


FLUX_KEYS = ((0, 0), (0, 1), (0, 2), (1, 0), (2, 0))
DIST_KEYS = ((0, 0), (0, 1), (0, 2), (0, 3), (1, 0), (1, 1), (1, 2), (2, 0), (2, 1), (3, 0))


def grow(carry, keys, sums, second):
    powers = [None, second, second * second, second * second * second]
    return tuple(
        c + (sums[i] if j == 0 else sums[i] * powers[j]) for c, (i, j) in zip(carry, keys)
    )


def moment_kernel(place_ref, dist_ref, after_ref, dist_sum_ref, zero_ref, dist_acc):
    step = pl.program_id(0)
    cells = dist_ref.shape[1]

    @pl.when(step == 0)
    def _():
        dist_acc[...] = jnp.zeros_like(dist_acc)

    speeds = last_speeds()
    tiles = range(NODES // SUB)
    first = (place_ref[0] + step).astype(F32) - HALF
    for t in range(cells // LANES):
        lanes = slice(t * LANES, (t + 1) * LANES)

        def body(y, carry, lanes=lanes):
            second = y.astype(F32) - HALF
            rows = [pl.ds(pl.multiple_of(y * NODES + j * SUB, SUB), SUB) for j in tiles]
            own = [dist_ref[r, lanes] for r in rows]
            return grow(carry, DIST_KEYS, z_sums(own, speeds, 4), second)

        zero = jnp.zeros((SUB, LANES), F32)
        part = lax.fori_loop(0, NODES, body, (zero,) * len(DIST_KEYS), unroll=4)
        s = dict(zip(DIST_KEYS, part))
        square = first * first
        add_rows(
            dist_acc,
            rest_of_moments(s, first)
            + [
                square * s[0, 0], s[0, 2], s[2, 0],
                first * s[0, 1], first * s[1, 0], s[1, 1],
                first * (square * s[0, 0] + s[0, 2] + s[2, 0]),
                square * s[0, 1] + s[0, 3] + s[2, 1],
                square * s[1, 0] + s[1, 2] + s[3, 0],
            ],
            lanes,
        )

    @pl.when(step == pl.num_programs(0) - 1)
    def _():
        dist_sum_ref[...] = jnp.concatenate(
            sum_rows(dist_acc, 14) + [jnp.zeros((2, cells), F32)], axis=0
        )
        zero_ref[...] = jnp.zeros_like(zero_ref)


def speeds_at(index):
    first = jnp.floor((index + 0.5) * (1.0 / PLANE))
    rest = index - PLANE * first
    second = jnp.floor((rest + 0.5) * (1.0 / NODES))
    return first - HALF, second - HALF, rest - NODES * second - HALF


def face_kernel(
    rows, start, place_ref, time_ref, index_ref, normal_ref, stream_ref, dist_ref, turned_ref,
    volume_ref, before_ref, pair_ref, cross_ref, ahead_ref, back_ref, *refs,
):
    moved_ref, flux_sum_ref, table_ref, flux_ref, flux_acc, ratio_ref = refs[-6:]
    cells, width = dist_ref.shape[1], pair_ref.shape[1]
    odd = place_ref[1]

    table_ref[0 : cells * SUB, :] = turned_ref[0]
    for block_ref, slot in ((pair_ref, 1 - odd), (cross_ref, odd), (ahead_ref, 2), (back_ref, 3)):
        for s in range(cross_ref.shape[0]):
            base = (cells + slot * width) * SUB + s
            table_ref[pl.ds(base, width, stride=SUB), :] = block_ref[s]
    inflow = cells + 4 * width
    table_ref[inflow * SUB : (inflow + 1) * SUB, :] = stream_ref[...]

    at = lax.broadcasted_iota(jnp.int32, (SUB, LANES), 0) * LANES
    at = at + lax.broadcasted_iota(jnp.int32, (SUB, LANES), 1) + (place_ref[0] * PLANE + start)
    speeds = speeds_at(at.astype(F32))

    @pl.loop(0, cells, unroll=4)
    def _(c):
        own = table_ref[pl.ds(pl.multiple_of(c * SUB, SUB), SUB), :]
        acc = low = full = None
        for k in range(FACES):
            source = pl.ds(pl.multiple_of(index_ref[k, c], SUB), SUB)
            normal = [normal_ref[3 * k + a, c] for a in range(3)]
            speed = speeds[0] * normal[0] + speeds[1] * normal[1] + speeds[2] * normal[2]
            inward = jnp.minimum(speed, 0.0)
            part = inward * table_ref[source, :]
            acc = part if k == 0 else acc + part
            low = inward if k == 0 else low + inward
            full = speed if k == 0 else full + speed
        flux_ref[pl.ds(pl.multiple_of(c * SUB, SUB), SUB), :] = acc + (full - low) * own

    ratio_ref[...] = rows8(time_ref[0, 0] / volume_ref[...])
    flux_acc[...] = jnp.zeros_like(flux_acc)
    for s in range(cross_ref.shape[0]):
        for t in range(cells // LANES):
            lanes = slice(t * LANES, (t + 1) * LANES)
            block = flux_ref[pl.ds(t * LANES * SUB + s, LANES, stride=SUB), :].T
            ratio = ratio_ref[:, lanes]
            sums = [None] * 5
            for r in range(LANES // SUB):
                row = s * LANES + r * SUB
                flux = block[r * SUB : (r + 1) * SUB, :]
                moved_ref[row : row + SUB, lanes] = dist_ref[row : row + SUB, lanes] - ratio * flux
                if start + row >= rows:
                    continue
                index = lax.broadcasted_iota(jnp.int32, (SUB, LANES), 0) + (
                    place_ref[0] * PLANE + start + row
                )
                c = speeds_at(index.astype(F32))
                square = 0.5 * (c[0] * c[0] + c[1] * c[1] + c[2] * c[2])
                parts = [flux, c[0] * flux, c[1] * flux, c[2] * flux, square * flux]
                sums = [p if q is None else q + p for q, p in zip(sums, parts)]
            if sums[0] is not None:
                add_rows(flux_acc, sums, lanes)
    flux_sum_ref[...] = before_ref[...] + jnp.concatenate(
        sum_rows(flux_acc, 5) + [jnp.zeros((3, cells), F32)], axis=0
    )


def hydrodynamic_variables(moments):
    density = moments[0]
    mean = [moments[1 + axis] / density for axis in range(3)]
    square = mean[0] ** 2 + mean[1] ** 2 + mean[2] ** 2
    return density, mean, (2.0 * moments[4] / density - square) / 3.0


def relax_kernel(
    planes, place_ref, time_ref, moved_ref, dist_sum_ref, flux_sum_ref, volume_ref, out_ref,
    x_ref, y_ref, z_ref, cell_ref,
):
    step = pl.program_id(0)
    cells = moved_ref.shape[1]

    @pl.when(step == 0)
    def _():
        time_step = time_ref[0, 0]
        ratio = time_step / volume_ref[...]
        sums = [dist_sum_ref[m : m + 1, :] for m in range(14)]
        density, mean, _ = hydrodynamic_variables(sums)
        xx, yy, zz, xy, xz, yz = sums[5:11]
        pairs = ((xx, xy, xz), (xy, yy, yz), (xz, yz, zz))
        square = mean[0] ** 2 + mean[1] ** 2 + mean[2] ** 2
        heat = []
        for a in range(3):
            cross = mean[0] * pairs[a][0] + mean[1] * pairs[a][1] + mean[2] * pairs[a][2]
            heat.append(
                0.5
                * (
                    sums[11 + a] - mean[a] * (2.0 * sums[4]) - 2.0 * cross
                    + 2.0 * mean[a] * square * density
                )
            )
        new = [sums[m] - ratio * flux_sum_ref[m : m + 1, :] for m in range(5)]
        density, mean, temp = hydrodynamic_variables(new)
        relax_time = MU_REF * jnp.exp(OMEGA * jnp.log(temp)) / (density * temp)
        relax = time_step / relax_time
        keep = 1.0 / (1.0 + relax)
        root = lax.rsqrt(2.0 * math.pi * temp)
        front = relax * keep * density * root * root * root
        along = (1.0 - PRANDTL) / (5.0 * density * temp * temp)
        for m, row in enumerate((keep, mean[0], temp, heat[0] * along, front)):
            cell_ref[m * SUB : (m + 1) * SUB, :] = rows8(row)
        nodes = lax.broadcasted_iota(jnp.int32, (NODES, cells), 0).astype(F32) - HALF
        for a, ref in ((1, y_ref), (2, z_ref)):
            rel = nodes - mean[a]
            square = rel * rel / temp
            for i, table in enumerate((jnp.exp(-0.5 * square), square, rel * heat[a] * along)):
                if a == 2:
                    ref[i * NODES : (i + 1) * NODES, :] = table
                    continue
                for y in range(NODES):
                    ref[i, y] = rows8(table[y : y + 1, :])

    keep, mean, temp, heat, front = [
        cell_ref[m * SUB : (m + 1) * SUB, :] for m in range(5)
    ]
    for p in range(planes):
        rel = (place_ref[0] + step * planes + p).astype(F32) - HALF - mean
        square = rel * rel / temp
        x_ref[0] = front * jnp.exp(-0.5 * square)
        x_ref[1] = square - 5.0
        x_ref[2] = rel * heat

        @pl.loop(0, NODES, unroll=2)
        def _(y, p=p):
            for t in range(cells // LANES):
                lanes = slice(t * LANES, (t + 1) * LANES)
                peak = x_ref[0, :, lanes] * y_ref[0, y, :, lanes]
                square = x_ref[1, :, lanes] + y_ref[1, y, :, lanes]
                along = x_ref[2, :, lanes] + y_ref[2, y, :, lanes]
                for j in range(NODES // SUB):
                    row = pl.ds(pl.multiple_of(p * PLANE + y * NODES + j * SUB, SUB), SUB)
                    z = [
                        z_ref[i * NODES + j * SUB : i * NODES + (j + 1) * SUB, lanes]
                        for i in range(3)
                    ]
                    shape = (along + z[2]) * (square + z[1]) + 1.0
                    moved = moved_ref[row, lanes] * cell_ref[0:SUB, lanes]
                    out_ref[row, lanes] = moved + peak * z[0] * shape


def params():
    return pltpu.CompilerParams(
        vmem_limit_bytes=VMEM_LIMIT, dimension_semantics=("arbitrary",)
    )


def whole(*shape):
    return pl.BlockSpec(shape, lambda i: (0,) * len(shape))


def planes_from(first, width, planes=1):
    return pl.BlockSpec((planes * PLANE, width), lambda i: (first // planes + i, 0))


SMEM = pl.BlockSpec(memory_space=pltpu.SMEM)
ANY = pl.BlockSpec(memory_space=pl.ANY)


def first_sends(place, lists, dist):
    cells, width = dist.shape[1], lists.shape[1]
    tiles = tiles_of(dist.shape[0], 0)
    block = SUB * LANES
    return pl.pallas_call(
        first_send_kernel,
        grid=(1,),
        in_specs=[SMEM, SMEM, pl.BlockSpec((block, cells), lambda i: (0, 0))],
        out_specs=[whole(tiles, width, LANES)] * 3,
        out_shape=[jax.ShapeDtypeStruct((tiles, width, LANES), F32)] * 3,
        scratch_shapes=[pltpu.VMEM((cells * SUB, LANES), F32), pltpu.VMEM((width * SUB, LANES), F32)],
        compiler_params=params(),
        cost_estimate=pl.CostEstimate(
            flops=0, bytes_accessed=4 * block * (cells + 3 * width), transcendentals=0
        ),
        name="first_sends",
    )(place, lists, dist)


def turned_cells(place, lists, dist, after):
    (rows, cells), width = dist.shape, lists.shape[1]
    block = SUB * LANES
    rounds = -(-rows // block)
    return pl.pallas_call(
        turn_kernel,
        grid=(rounds,),
        in_specs=[SMEM, SMEM, pl.BlockSpec((block, cells), lambda i: (i, 0)), ANY],
        out_specs=[
            pl.BlockSpec((1, cells * SUB, LANES), lambda i: (i, 0, 0)),
            pl.BlockSpec((SUB, width, LANES), lambda i: (i, 0, 0)),
        ],
        out_shape=[
            jax.ShapeDtypeStruct((rounds, cells * SUB, LANES), F32),
            jax.ShapeDtypeStruct((-(-rows // LANES), width, LANES), F32),
        ],
        scratch_shapes=[pltpu.VMEM((width * SUB, LANES), F32)],
        compiler_params=params(),
        cost_estimate=pl.CostEstimate(
            flops=0, bytes_accessed=4 * rows * (2 * cells + width), transcendentals=0
        ),
        name="turned_cells",
    )(place, lists, dist, after)


def later_sends(place, lists, turned, i, tiles, after):
    height, width = turned.shape[1], lists.shape[1]
    return pl.pallas_call(
        send_kernel,
        grid=(1,),
        in_specs=[SMEM, SMEM, pl.BlockSpec((1, height, LANES), lambda _: (i, 0, 0)), ANY],
        out_specs=[whole(tiles, width, LANES)] * 3,
        out_shape=[jax.ShapeDtypeStruct((tiles, width, LANES), F32)] * 3,
        scratch_shapes=[pltpu.VMEM((width * SUB, LANES), F32)],
        compiler_params=params(),
        cost_estimate=pl.CostEstimate(
            flops=0, bytes_accessed=4 * LANES * (height + 3 * tiles * width), transcendentals=0
        ),
        name="later_sends",
    )(place, lists, turned, after)


def dist_moments(place, dist, after):
    rows, cells = dist.shape
    return pl.pallas_call(
        moment_kernel,
        grid=(rows // PLANE,),
        in_specs=[SMEM, planes_from(0, cells), ANY],
        out_specs=[whole(16, cells), whole(8, cells)],
        out_shape=[
            jax.ShapeDtypeStruct((16, cells), F32),
            jax.ShapeDtypeStruct((8, cells), F32),
        ],
        scratch_shapes=[pltpu.VMEM((14 * SUB, cells), F32)],
        compiler_params=params(),
        cost_estimate=pl.CostEstimate(
            flops=30 * rows * cells, bytes_accessed=4 * rows * cells, transcendentals=0
        ),
        name="dist_moments",
    )(place, dist, after)


def face_sums(place, time_step, index, normals, stream, dist, turned, volume, before, moved, pair, arrived, i):
    rows, cells = dist.shape
    width = pair.shape[1]
    tiles = arrived[0].shape[0]
    block = SUB * LANES
    extra, aliases = ((), {}) if moved is None else ((moved,), {13: 0})
    return pl.pallas_call(
        functools.partial(face_kernel, rows, i * block),
        grid=(1,),
        in_specs=[
            SMEM, SMEM, SMEM, SMEM,
            pl.BlockSpec((SUB, LANES), lambda _: (i, 0)),
            pl.BlockSpec((block, cells), lambda _: (i, 0)),
            pl.BlockSpec((1, cells * SUB, LANES), lambda _: (i, 0, 0)),
            whole(1, cells), whole(8, cells),
            pl.BlockSpec((SUB, width, LANES), lambda _: (i, 0, 0)),
        ]
        + [whole(tiles, width, LANES)] * 3
        + [ANY] * len(extra),
        out_specs=[pl.BlockSpec((block, cells), lambda _: (i, 0)), whole(8, cells)],
        out_shape=[
            jax.ShapeDtypeStruct((rows, cells), F32),
            jax.ShapeDtypeStruct((8, cells), F32),
        ],
        scratch_shapes=[
            pltpu.VMEM(((cells + 4 * width + 1) * SUB, LANES), F32),
            pltpu.VMEM((cells * SUB, LANES), F32),
            pltpu.VMEM((5 * SUB, cells), F32),
            pltpu.VMEM((SUB, cells), F32),
        ],
        input_output_aliases=aliases,
        compiler_params=params(),
        cost_estimate=pl.CostEstimate(
            flops=70 * block * cells,
            bytes_accessed=4 * block * (3 * cells + 4 * width),
            transcendentals=0,
        ),
        name="face_sums",
    )(place, time_step, index, normals, stream, dist, turned, volume, before, pair, *arrived, *extra)


def step_planes(planes):
    return 2 - planes % 2


def relaxed(place, time_step, moved, dist_sum, flux_sum, volume):
    rows, cells = moved.shape
    planes = step_planes(rows // PLANE)
    return pl.pallas_call(
        functools.partial(relax_kernel, planes),
        grid=(rows // PLANE // planes,),
        in_specs=[
            SMEM, SMEM, planes_from(0, cells, planes), whole(16, cells), whole(8, cells),
            whole(1, cells),
        ],
        out_specs=planes_from(0, cells, planes),
        out_shape=jax.ShapeDtypeStruct((rows, cells), F32),
        scratch_shapes=[
            pltpu.VMEM((3, SUB, cells), F32),
            pltpu.VMEM((3, NODES, SUB, cells), F32),
            pltpu.VMEM((3 * NODES, cells), F32),
            pltpu.VMEM((5 * SUB, cells), F32),
        ],
        compiler_params=params(),
        cost_estimate=pl.CostEstimate(
            flops=10 * rows * cells, bytes_accessed=8 * rows * cells, transcendentals=0
        ),
        name="relaxed",
    )(place, time_step, moved, dist_sum, flux_sum, volume)


def local(dist, free_stream, area_normal, cell_volume, face_nbr, face_type, send_list):
    rows, cells = dist.shape
    planes = rows // PLANE
    dirs, width = send_list.shape
    block = SUB * LANES
    rounds = -(-rows // block)
    place = jnp.stack([lax.axis_index("vel") * planes, lax.axis_index("space") % 2]).astype(jnp.int32)

    def sent(blocks):
        return (
            swapped(blocks[0], "space", 1),
            passed_along(blocks[1], "space", neighbour_steps[2]),
            passed_along(blocks[2], "space", neighbour_steps[3]),
        )

    blocks = first_sends(place, send_list, dist)
    arrived = [sent(blocks)]
    turned, pair = turned_cells(place, send_list, dist, blocks[0])
    pair = swapped(pair, "space", 0)
    if rounds > 1:
        arrived.append(sent(later_sends(place, send_list, turned, 1, tiles_of(rows, 1), turned)))

    top_speed = HALF * math.sqrt(3.0)
    normals = area_normal.reshape(FACES, 3, cells)
    face_areas = jnp.sqrt(jnp.sum(normals * normals, axis=1))
    cell_limit = cell_volume / (top_speed * jnp.sum(face_areas, axis=0))
    least = jnp.min(cell_limit).reshape(1, 1)
    shift = 1
    while shift < lax.axis_size("space"):
        least = jnp.minimum(least, passed_along(least, "space", shift))
        shift *= 2
    time_step = CFL * least

    own = jnp.arange(cells, dtype=jnp.int32)[None, :]
    inflow = cells + dirs * width
    index = jnp.where(face_type == 0, face_nbr, jnp.where(face_type == 1, inflow, own)) * SUB
    volume = cell_volume.reshape(1, cells)
    stream = jnp.pad(free_stream, (0, rounds * block - rows)).reshape(rounds * SUB, LANES)
    dist_sum, flux_sum = dist_moments(place, dist, turned)
    dist_sum = summed_over(dist_sum, "vel")
    moved = None
    for i in range(rounds):
        moved, flux_sum = face_sums(
            place, time_step, index, area_normal, stream, dist, turned, volume, flux_sum, moved,
            pair, arrived[i], i,
        )
        if i + 2 < rounds:
            blocks = later_sends(place, send_list, turned, i + 2, tiles_of(rows, i + 2), flux_sum)
            arrived.append(sent(blocks))
    flux_sum = summed_over(flux_sum, "vel")
    return relaxed(place, time_step, moved, dist_sum, flux_sum, volume)


def solution(mesh):
    return jax.shard_map(
        local,
        mesh=mesh,
        in_specs=(
            P("vel", "space"),
            P("vel"),
            P(None, "space"),
            P("space"),
            P(None, "space"),
            P(None, "space"),
            P(None, "space"),
        ),
        out_specs=P("vel", "space"),
        check_vma=False,
    )
```

```python
import functools
import math

import jax
import jax.numpy as jnp
from jax import lax
from jax.experimental import pallas as pl
from jax.experimental.pallas import tpu as pltpu
from jax.sharding import PartitionSpec as P

NODES = 24
PLANE = NODES * NODES
HALF = (NODES - 1) / 2.0
FACES = 6
CFL = 0.9
MU_REF = 60.0
OMEGA = 0.81
PRANDTL = 2.0 / 3.0
neighbour_steps = (1, -1, 2, -2)

LANES = 128
SUB = 8
F32 = jnp.float32
VMEM_LIMIT = 63_400_000


def passed_along(block, axis, distance):
    count = lax.axis_size(axis)
    route = [((i - distance) % count, i) for i in range(count)]
    return lax.ppermute(block, axis, route)


def swapped(block, axis, start):
    count = lax.axis_size(axis)
    route = []
    for i in range(start, start + count, 2):
        route += [(i % count, (i + 1) % count), ((i + 1) % count, i % count)]
    return lax.ppermute(block, axis, route)


def summed_over(value, axis):
    count = lax.axis_size(axis)
    if count & (count - 1):
        return lax.psum(value, axis)
    reach = 1
    while reach < count:
        value = value + lax.ppermute(value, axis, [(i, i ^ reach) for i in range(count)])
        reach *= 2
    return value


def round_plan(rows):
    tiles = -(-rows // LANES)
    groups = -(-tiles // SUB)
    sizes = [1, 1] if groups > 2 else []
    sizes += [2] * max(0, (groups - len(sizes) - 1) // 2)
    sizes += [1] * (groups - sum(sizes))
    plan, first = [], 0
    for size in sizes:
        plan.append((first, size, min(size * SUB, tiles - first * SUB)))
        first += size
    return plan


def turn(dist_ref, turned_ref):
    cells = dist_ref.shape[1]
    for s in range(SUB):
        for t in range(cells // LANES):
            block = dist_ref[s * LANES : (s + 1) * LANES, t * LANES : (t + 1) * LANES]
            turned_ref[pl.ds(t * LANES * SUB + s, LANES, stride=SUB), :] = block.T


def pick_rows(list_ref, row, turned_ref, picked_ref, out_ref, tiles):
    width = out_ref.shape[1]

    @pl.loop(0, width, unroll=8)
    def _(j):
        source = pl.ds(pl.multiple_of(list_ref[row, j] * SUB, SUB), SUB)
        picked_ref[pl.ds(pl.multiple_of(j * SUB, SUB), SUB), :] = turned_ref[source, :]

    for s in range(tiles):
        out_ref[s] = picked_ref[pl.ds(s, width, stride=SUB), :]


def first_send_kernel(
    place_ref, list_ref, dist_ref, normal_ref, volume_ref, cross_ref, ahead_ref, back_ref, least_ref,
    turned_ref, picked_ref,
):
    turn(dist_ref, turned_ref)
    for row, out_ref in ((2, ahead_ref), (3, back_ref), (1 - place_ref[1], cross_ref)):
        pick_rows(list_ref, row, turned_ref, picked_ref, out_ref, out_ref.shape[0])
    area = jnp.zeros_like(volume_ref)
    for k in range(FACES):
        part = [normal_ref[3 * k + a : 3 * k + a + 1, :] for a in range(3)]
        area = area + jnp.sqrt(part[0] * part[0] + part[1] * part[1] + part[2] * part[2])
    limit = volume_ref[...] / (HALF * math.sqrt(3.0) * area)
    least_ref[...] = jnp.broadcast_to(jnp.min(limit, axis=1, keepdims=True), least_ref.shape)


def turn_kernel(
    plan, place_ref, list_ref, dist_ref, after_ref, turned_ref, pair_ref, *refs,
):
    outs, picked_ref = refs[:-1], refs[-1]
    step = pl.program_id(0)
    turn(dist_ref, turned_ref.at[0])
    pick_rows(list_ref, place_ref[1], turned_ref.at[0], picked_ref, pair_ref, SUB)
    for i, (first, groups, tiles) in enumerate(plan):
        for g in range(groups):

            @pl.when(step == first + g)
            def _(i=i, g=g, tiles=tiles):
                here = min(SUB, tiles - g * SUB)
                for row, out_ref in zip((1 - place_ref[1], 2, 3), outs[3 * i : 3 * i + 3]):
                    pick_rows(list_ref, row, turned_ref.at[0], picked_ref, out_ref, here)


def rows8(row):
    return jnp.broadcast_to(row, (SUB, row.shape[-1]))


def last_speeds():
    index = lax.broadcasted_iota(jnp.int32, (SUB, LANES), 0).astype(F32) - HALF
    return [index + float(j * SUB) for j in range(NODES // SUB)]


def z_sums(tiles, speeds, powers):
    sums, terms = [], list(tiles)
    for p in range(powers):
        if p:
            terms = [t * c for t, c in zip(terms, speeds)]
        sums.append(terms[0] + terms[1] + terms[2])
    return sums


def rest_of_moments(sums, first):
    energy = 0.5 * (first * first * sums[0, 0] + sums[0, 1 + 1] + sums[2, 0])
    return [sums[0, 0], first * sums[0, 0], sums[0, 1], sums[1, 0], energy]


def add_rows(acc_ref, values, lanes):
    for m, value in enumerate(values):
        acc_ref[m * SUB : (m + 1) * SUB, lanes] += value


def sum_rows(acc_ref, count):
    return [jnp.sum(acc_ref[m * SUB : (m + 1) * SUB, :], axis=0, keepdims=True) for m in range(count)]


FLUX_KEYS = ((0, 0), (0, 1), (0, 2), (1, 0), (2, 0))
DIST_KEYS = ((0, 0), (0, 1), (0, 2), (0, 3), (1, 0), (1, 1), (1, 2), (2, 0), (2, 1), (3, 0))


def grow(carry, keys, sums, second):
    powers = [None, second, second * second, second * second * second]
    return tuple(
        c + (sums[i] if j == 0 else sums[i] * powers[j]) for c, (i, j) in zip(carry, keys)
    )


def moment_kernel(place_ref, dist_ref, after_ref, dist_sum_ref, dist_acc):
    step = pl.program_id(0)
    cells = dist_ref.shape[1]

    @pl.when(step == 0)
    def _():
        dist_acc[...] = jnp.zeros_like(dist_acc)

    speeds = last_speeds()
    tiles = range(NODES // SUB)
    first = (place_ref[0] + step).astype(F32) - HALF
    for t in range(cells // LANES):
        lanes = slice(t * LANES, (t + 1) * LANES)

        def body(y, carry, lanes=lanes):
            second = y.astype(F32) - HALF
            rows = [pl.ds(pl.multiple_of(y * NODES + j * SUB, SUB), SUB) for j in tiles]
            own = [dist_ref[r, lanes] for r in rows]
            return grow(carry, DIST_KEYS, z_sums(own, speeds, 4), second)

        zero = jnp.zeros((SUB, LANES), F32)
        part = lax.fori_loop(0, NODES, body, (zero,) * len(DIST_KEYS), unroll=4)
        s = dict(zip(DIST_KEYS, part))
        square = first * first
        add_rows(
            dist_acc,
            rest_of_moments(s, first)
            + [
                square * s[0, 0], s[0, 2], s[2, 0],
                first * s[0, 1], first * s[1, 0], s[1, 1],
                first * (square * s[0, 0] + s[0, 2] + s[2, 0]),
                square * s[0, 1] + s[0, 3] + s[2, 1],
                square * s[1, 0] + s[1, 2] + s[3, 0],
            ],
            lanes,
        )

    @pl.when(step == pl.num_programs(0) - 1)
    def _():
        dist_sum_ref[...] = jnp.concatenate(
            sum_rows(dist_acc, 14) + [jnp.zeros((2, cells), F32)], axis=0
        )


def speeds_at(index):
    first = jnp.floor((index + 0.5) * (1.0 / PLANE))
    rest = index - PLANE * first
    second = jnp.floor((rest + 0.5) * (1.0 / NODES))
    return first - HALF, second - HALF, rest - NODES * second - HALF


def time_row(least_ref, cells):
    return CFL * jnp.concatenate([least_ref[0:1, :]] * (cells // LANES), axis=1)


def face_kernel(
    rows, start, groups, rounds, place_ref, index_ref, normal_ref, stream_ref, turned_ref,
    before_ref, *refs,
):
    pairs, refs = refs[:groups], refs[groups:]
    received = [refs[3 * i : 3 * i + 3] for i in range(len(rounds))]
    flux_out_ref, flux_sum_ref, table_ref, flux_ref, flux_acc = refs[-5:]
    cells, width = flux_out_ref.shape[1], pairs[0].shape[1]
    odd = place_ref[1]
    block = SUB * LANES
    place_of, tiles = [], 0
    for i, count in enumerate(rounds):
        for g in range(count):
            place_of.append((received[i], g, min(SUB, received[i][0].shape[0] - g * SUB)))
            tiles += place_of[-1][2]

    speeds = []
    for g in range(groups):
        table_ref[g, 0 : cells * SUB, :] = turned_ref[g]
        (cross_ref, ahead_ref, back_ref), h, count = place_of[g]
        sources = ((pairs[g], 0, 1 - odd), (cross_ref, h, odd), (ahead_ref, h, 2), (back_ref, h, 3))
        for block_ref, part, slot in sources:
            for s in range(count):
                base = (cells + slot * width) * SUB + s
                table_ref[g, pl.ds(base, width, stride=SUB), :] = block_ref[part * SUB + s]
        inflow = cells + 4 * width
        table_ref[g, inflow * SUB : (inflow + 1) * SUB, :] = stream_ref[g * SUB : (g + 1) * SUB, :]
        at = lax.broadcasted_iota(jnp.int32, (SUB, LANES), 0) * LANES
        at = at + lax.broadcasted_iota(jnp.int32, (SUB, LANES), 1)
        at = at + (place_ref[0] * PLANE + start + g * block)
        speeds.append(speeds_at(at.astype(F32)))

    @pl.loop(0, cells, unroll=4)
    def _(c):
        here = pl.ds(pl.multiple_of(c * SUB, SUB), SUB)
        acc, low, full = ([None] * groups for _ in range(3))
        for k in range(FACES):
            source = pl.ds(pl.multiple_of(index_ref[k, c], SUB), SUB)
            normal = [normal_ref[3 * k + a, c] for a in range(3)]
            for g in range(groups):
                speed = sum(speeds[g][a] * normal[a] for a in range(1, 3)) + speeds[g][0] * normal[0]
                inward = jnp.minimum(speed, 0.0)
                part = inward * table_ref[g, source, :]
                acc[g] = part if k == 0 else acc[g] + part
                low[g] = inward if k == 0 else low[g] + inward
                full[g] = speed if k == 0 else full[g] + speed
        for g in range(groups):
            flux_ref[g, here, :] = acc[g] + (full[g] - low[g]) * table_ref[g, here, :]

    flux_acc[...] = jnp.zeros_like(flux_acc)
    parts = [slice(t * LANES, (t + 1) * LANES) for t in range(cells // LANES)]
    for q in range(tiles):
        g, s = divmod(q, SUB)
        turned = [
            flux_ref[g, pl.ds(t * LANES * SUB + s, LANES, stride=SUB), :].T for t in range(len(parts))
        ]
        sums = [[None] * 5 for _ in parts]
        for r in range(LANES // SUB):
            row = q * LANES + r * SUB
            counted = start + row < rows
            index = lax.broadcasted_iota(jnp.int32, (SUB, LANES), 0) + (
                place_ref[0] * PLANE + start + row
            )
            c = speeds_at(index.astype(F32))
            square = 0.5 * (c[0] * c[0] + c[1] * c[1] + c[2] * c[2])
            for t, lanes in enumerate(parts):
                flux = turned[t][r * SUB : (r + 1) * SUB, :]
                flux_out_ref[row : row + SUB, lanes] = flux
                if counted:
                    terms = [flux, c[0] * flux, c[1] * flux, c[2] * flux, square * flux]
                    sums[t] = [p if z is None else z + p for z, p in zip(sums[t], terms)]
        for t, lanes in enumerate(parts):
            if sums[t][0] is not None:
                add_rows(flux_acc, sums[t], lanes)
    flux_sum_ref[...] = before_ref[...] + jnp.concatenate(
        sum_rows(flux_acc, 5) + [jnp.zeros((3, cells), F32)], axis=0
    )


def hydrodynamic_variables(moments):
    density = moments[0]
    mean = [moments[1 + axis] / density for axis in range(3)]
    square = mean[0] ** 2 + mean[1] ** 2 + mean[2] ** 2
    return density, mean, (2.0 * moments[4] / density - square) / 3.0


def relax_kernel(
    planes, place_ref, least_ref, dist_ref, flux_ref, dist_sum_ref, flux_sum_ref, volume_ref, out_ref,
    x_ref, y_ref, z_ref, cell_ref,
):
    step = pl.program_id(0)
    cells = dist_ref.shape[1]

    @pl.when(step == 0)
    def _():
        time_step = time_row(least_ref, cells)
        ratio = time_step / volume_ref[...]
        sums = [dist_sum_ref[m : m + 1, :] for m in range(14)]
        density, mean, _ = hydrodynamic_variables(sums)
        xx, yy, zz, xy, xz, yz = sums[5:11]
        pairs = ((xx, xy, xz), (xy, yy, yz), (xz, yz, zz))
        square = mean[0] ** 2 + mean[1] ** 2 + mean[2] ** 2
        heat = []
        for a in range(3):
            cross = mean[0] * pairs[a][0] + mean[1] * pairs[a][1] + mean[2] * pairs[a][2]
            heat.append(
                0.5
                * (
                    sums[11 + a] - mean[a] * (2.0 * sums[4]) - 2.0 * cross
                    + 2.0 * mean[a] * square * density
                )
            )
        new = [sums[m] - ratio * flux_sum_ref[m : m + 1, :] for m in range(5)]
        density, mean, temp = hydrodynamic_variables(new)
        relax_time = MU_REF * jnp.exp(OMEGA * jnp.log(temp)) / (density * temp)
        relax = time_step / relax_time
        keep = 1.0 / (1.0 + relax)
        root = lax.rsqrt(2.0 * math.pi * temp)
        front = relax * keep * density * root * root * root
        along = (1.0 - PRANDTL) / (5.0 * density * temp * temp)
        for m, row in enumerate((keep, mean[0], temp, heat[0] * along, front, keep * ratio)):
            cell_ref[m * SUB : (m + 1) * SUB, :] = rows8(row)
        nodes = lax.broadcasted_iota(jnp.int32, (NODES, cells), 0).astype(F32) - HALF
        for a, ref in ((1, y_ref), (2, z_ref)):
            rel = nodes - mean[a]
            square = rel * rel / temp
            for i, table in enumerate((jnp.exp(-0.5 * square), square, rel * heat[a] * along)):
                if a == 2:
                    ref[i * NODES : (i + 1) * NODES, :] = table
                    continue
                for y in range(NODES):
                    ref[i, y] = rows8(table[y : y + 1, :])

    keep, mean, temp, heat, front = [
        cell_ref[m * SUB : (m + 1) * SUB, :] for m in range(5)
    ]
    for p in range(planes):
        rel = (place_ref[0] + step * planes + p).astype(F32) - HALF - mean
        square = rel * rel / temp
        x_ref[0] = front * jnp.exp(-0.5 * square)
        x_ref[1] = square - 5.0
        x_ref[2] = rel * heat

        for t in range(cells // LANES):
            lanes = slice(t * LANES, (t + 1) * LANES)
            from_x = [x_ref[i, :, lanes] for i in range(3)]
            tiles = range(NODES // SUB)
            from_z = [
                [z_ref[i * NODES + j * SUB : i * NODES + (j + 1) * SUB, lanes] for j in tiles]
                for i in range(3)
            ]
            share, flow = cell_ref[0:SUB, lanes], cell_ref[5 * SUB : 6 * SUB, lanes]

            @pl.loop(0, NODES, unroll=4)
            def _(y, p=p, lanes=lanes, from_x=from_x, from_z=from_z, share=share, flow=flow):
                peak = from_x[0] * y_ref[0, y, :, lanes]
                square = from_x[1] + y_ref[1, y, :, lanes]
                along = from_x[2] + y_ref[2, y, :, lanes]
                for j in range(NODES // SUB):
                    row = pl.ds(pl.multiple_of(p * PLANE + y * NODES + j * SUB, SUB), SUB)
                    moved = dist_ref[row, lanes] * share - flux_ref[row, lanes] * flow
                    shape = (along + from_z[2][j]) * (square + from_z[1][j]) + 1.0
                    out_ref[row, lanes] = moved + peak * from_z[0][j] * shape


def params():
    return pltpu.CompilerParams(
        vmem_limit_bytes=VMEM_LIMIT, dimension_semantics=("arbitrary",)
    )


def whole(*shape):
    return pl.BlockSpec(shape, lambda i: (0,) * len(shape))


def planes_from(first, width, planes=1):
    return pl.BlockSpec((planes * PLANE, width), lambda i: (first // planes + i, 0))


SMEM = pl.BlockSpec(memory_space=pltpu.SMEM)
ANY = pl.BlockSpec(memory_space=pl.ANY)


def hint(amount):
    return pl.CostEstimate(flops=0, bytes_accessed=amount, transcendentals=0)


def gate_kernel(*refs):
    pass


def gated(blocks, after):
    blocks = list(blocks)
    return pl.pallas_call(
        gate_kernel,
        in_specs=[ANY] * (len(blocks) + len(after)),
        out_specs=[ANY] * len(blocks),
        out_shape=[jax.ShapeDtypeStruct(block.shape, block.dtype) for block in blocks],
        input_output_aliases={i: i for i in range(len(blocks))},
        cost_estimate=hint(0),
        name="gate",
    )(*blocks, *after)


def first_sends(place, lists, dist, normals, volume, tiles):
    cells, width = dist.shape[1], lists.shape[1]
    return pl.pallas_call(
        first_send_kernel,
        grid=(1,),
        in_specs=[
            SMEM, SMEM, pl.BlockSpec((SUB * LANES, cells), lambda i: (0, 0)),
            whole(3 * FACES, cells), whole(1, cells),
        ],
        out_specs=[whole(tiles, width, LANES)] * 3 + [whole(SUB, LANES)],
        out_shape=[jax.ShapeDtypeStruct((tiles, width, LANES), F32)] * 3
        + [jax.ShapeDtypeStruct((SUB, LANES), F32)],
        scratch_shapes=[pltpu.VMEM((cells * SUB, LANES), F32), pltpu.VMEM((width * SUB, LANES), F32)],
        compiler_params=params(),
        cost_estimate=hint(4096),
        name="first_sends",
    )(place, lists, dist, normals, volume)


def turned_cells(place, lists, dist, plan, after):
    (rows, cells), width = dist.shape, lists.shape[1]
    block = SUB * LANES
    rounds = -(-rows // block)

    def part_of(first, groups):
        return pl.BlockSpec(
            (SUB, width, LANES), lambda i: (jnp.clip(i - first, 0, groups - 1), 0, 0)
        )

    outs = [(part_of(first, groups), tiles) for first, groups, tiles in plan for _ in range(3)]
    return pl.pallas_call(
        functools.partial(turn_kernel, plan),
        grid=(rounds,),
        in_specs=[
            SMEM, SMEM, pl.BlockSpec((block, cells), lambda i: (i, 0)), ANY,
        ],
        out_specs=[
            pl.BlockSpec((1, cells * SUB, LANES), lambda i: (i, 0, 0)),
            pl.BlockSpec((SUB, width, LANES), lambda i: (i, 0, 0)),
        ]
        + [spec for spec, _ in outs],
        out_shape=[
            jax.ShapeDtypeStruct((rounds, cells * SUB, LANES), F32),
            jax.ShapeDtypeStruct((-(-rows // LANES), width, LANES), F32),
        ]
        + [jax.ShapeDtypeStruct((tiles, width, LANES), F32) for _, tiles in outs],
        scratch_shapes=[pltpu.VMEM((width * SUB, LANES), F32)],
        compiler_params=params(),
        cost_estimate=hint(4096),
        name="turned_cells",
    )(place, lists, dist, after)


def dist_moments(place, dist, after):
    rows, cells = dist.shape
    return pl.pallas_call(
        moment_kernel,
        grid=(rows // PLANE,),
        in_specs=[SMEM, planes_from(0, cells), ANY],
        out_specs=whole(16, cells),
        out_shape=jax.ShapeDtypeStruct((16, cells), F32),
        scratch_shapes=[pltpu.VMEM((14 * SUB, cells), F32)],
        compiler_params=params(),
        cost_estimate=hint(4096),
        name="dist_moments",
    )(place, dist, after)


def face_sums(shape, place, index, normals, stream, turned, before, flux, pair, arrived, parts, after):
    (rows, cells), width = shape, pair.shape[1]
    first, counts = parts[0][0], [groups for _, groups, _ in parts]
    groups = sum(counts)
    block = SUB * LANES
    offset = first // groups
    extra = () if flux is None else (flux,)
    received = [block for group in arrived for block in group]
    aliases = {6 + groups + len(received): 0} if extra else {}
    return pl.pallas_call(
        functools.partial(face_kernel, rows, first * block, groups, counts),
        grid=(1,),
        in_specs=[
            SMEM, SMEM, SMEM,
            pl.BlockSpec((groups * SUB, LANES), lambda _: (offset, 0)),
            pl.BlockSpec((groups, cells * SUB, LANES), lambda _: (offset, 0, 0)),
            whole(8, cells),
        ]
        + [
            pl.BlockSpec((SUB, width, LANES), lambda _, g=g: (first + g, 0, 0))
            for g in range(groups)
        ]
        + [whole(*block.shape) for block in received]
        + [ANY] * (len(extra) + len(after)),
        out_specs=[
            pl.BlockSpec((groups * block, cells), lambda _: (offset, 0)), whole(8, cells),
        ],
        out_shape=[
            jax.ShapeDtypeStruct((rows, cells), F32),
            jax.ShapeDtypeStruct((8, cells), F32),
        ],
        scratch_shapes=[
            pltpu.VMEM((groups, (cells + 4 * width + 1) * SUB, LANES), F32),
            pltpu.VMEM((groups, cells * SUB, LANES), F32),
            pltpu.VMEM((5 * SUB, cells), F32),
        ],
        input_output_aliases=aliases,
        compiler_params=params(),
        cost_estimate=hint(4096),
        name="face_sums",
    )(place, index, normals, stream, turned, before, *([pair] * groups), *received, *extra, *after)


def step_planes(planes):
    return 2 - planes % 2


def relaxed(place, least, dist, flux, dist_sum, flux_sum, volume):
    rows, cells = dist.shape
    planes = step_planes(rows // PLANE)
    return pl.pallas_call(
        functools.partial(relax_kernel, planes),
        grid=(rows // PLANE // planes,),
        in_specs=[
            SMEM, whole(SUB, LANES), planes_from(0, cells, planes), planes_from(0, cells, planes),
            whole(16, cells), whole(8, cells), whole(1, cells),
        ],
        out_specs=planes_from(0, cells, planes),
        out_shape=jax.ShapeDtypeStruct((rows, cells), F32),
        scratch_shapes=[
            pltpu.VMEM((3, SUB, cells), F32),
            pltpu.VMEM((3, NODES, SUB, cells), F32),
            pltpu.VMEM((3 * NODES, cells), F32),
            pltpu.VMEM((6 * SUB, cells), F32),
        ],
        compiler_params=params(),
        cost_estimate=pl.CostEstimate(
            flops=10 * rows * cells, bytes_accessed=8 * rows * cells, transcendentals=0
        ),
        name="relaxed",
    )(place, least, dist, flux, dist_sum, flux_sum, volume)


def local(dist, free_stream, area_normal, cell_volume, face_nbr, face_type, send_list):
    rows, cells = dist.shape
    planes = rows // PLANE
    dirs, width = send_list.shape
    block = SUB * LANES
    rounds = -(-rows // block)
    place = jnp.stack([lax.axis_index("vel") * planes, lax.axis_index("space") % 2]).astype(jnp.int32)

    def sent(blocks):
        return (
            swapped(blocks[0], "space", 1),
            passed_along(blocks[1], "space", neighbour_steps[2]),
            passed_along(blocks[2], "space", neighbour_steps[3]),
        )

    plan = round_plan(rows)
    volume = cell_volume.reshape(1, cells)
    own = jnp.arange(cells, dtype=jnp.int32)[None, :]
    inflow = cells + dirs * width
    index = jnp.where(face_type == 0, face_nbr, jnp.where(face_type == 1, inflow, own)) * SUB
    stream = jnp.pad(free_stream, (0, rounds * block - rows)).reshape(rounds * SUB, LANES)

    shift, n_space = 1, lax.axis_size("space")
    *blocks, least = first_sends(place, send_list, dist, area_normal, volume, plan[0][2])
    turned, pair, *later = turned_cells(place, send_list, dist, plan[1:], blocks[0])
    arrived, pending, gate_after = [], [], []
    flux, flux_sum, dist_sum = None, jnp.zeros((8, cells), F32), None
    for i, part in enumerate(plan):
        arrived.append(sent(blocks))
        if shift < n_space:
            least = jnp.minimum(least, passed_along(least, "space", shift))
            shift *= 2
        if i == 0:
            gate_after = [turned]
        elif i == 1:
            pair = swapped(pair, "space", 0)
            dist_sum = dist_moments(place, dist, blocks[0])
            gate_after = [dist_sum, pair]
        else:
            parts = plan[0:2] if i == 2 else plan[i - 1 : i]
            flux, flux_sum = face_sums(
                dist.shape, place, index, area_normal, stream, turned, flux_sum, flux,
                pair, arrived[0:2] if i == 2 else arrived[i - 1 : i], parts, [blocks[0]],
            )
            gate_after = [flux_sum]
        if i == 2:
            dist_sum = summed_over(dist_sum, "vel")
            gate_after.append(dist_sum)
        if i + 1 < len(plan):
            blocks = later[3 * i : 3 * i + 3]
            rest = [least, pair] if i == 0 else [least]
            gated_arrays = gated([*blocks, *rest], [*arrived[-1], *gate_after])
            blocks, least = gated_arrays[:3], gated_arrays[3]
            if i == 0:
                pair = gated_arrays[4]
    if len(plan) == 1:
        dist_sum = dist_moments(place, dist, blocks[0])
        pair = swapped(pair, "space", 0)
    if len(plan) < 3:
        dist_sum = summed_over(dist_sum, "vel")
    done = 0 if len(plan) < 3 else len(plan) - 1
    flux, flux_sum = face_sums(
        dist.shape, place, index, area_normal, stream, turned, flux_sum, flux,
        pair, arrived[done:], plan[done:], [],
    )
    while shift < n_space:
        least = jnp.minimum(least, passed_along(least, "space", shift))
        shift *= 2
    flux_sum = summed_over(flux_sum, "vel")
    return relaxed(place, least, dist, flux, dist_sum, flux_sum, volume)


def solution(mesh):
    return jax.shard_map(
        local,
        mesh=mesh,
        in_specs=(
            P("vel", "space"),
            P("vel"),
            P(None, "space"),
            P("space"),
            P(None, "space"),
            P(None, "space"),
            P(None, "space"),
        ),
        out_specs=P("vel", "space"),
        check_vma=False,
    )
```

```python
import functools
import math

import jax
import jax.numpy as jnp
from jax import lax
from jax.experimental import pallas as pl
from jax.experimental.pallas import tpu as pltpu
from jax.sharding import PartitionSpec as P

NODES = 24
PLANE = NODES * NODES
HALF = (NODES - 1) / 2.0
FACES = 6
CFL = 0.9
MU_REF = 60.0
OMEGA = 0.81
PRANDTL = 2.0 / 3.0
neighbour_steps = (1, -1, 2, -2)

LANES = 128
SUB = 8
F32 = jnp.float32
VMEM_LIMIT = 66_900_000


def passed_along(block, axis, distance):
    count = lax.axis_size(axis)
    route = [((i - distance) % count, i) for i in range(count)]
    return lax.ppermute(block, axis, route)


def swapped(block, axis, start):
    count = lax.axis_size(axis)
    route = []
    for i in range(start, start + count, 2):
        route += [(i % count, (i + 1) % count), ((i + 1) % count, i % count)]
    return lax.ppermute(block, axis, route)


def halves_over(value, axis):
    count = lax.axis_size(axis)
    if count & (count - 1):
        return lax.psum(value, axis), jnp.zeros_like(value)
    reach, other = 1, jnp.zeros_like(value)
    while reach < count:
        value = value if reach == 1 else value + other
        other = lax.ppermute(value, axis, [(i, i ^ reach) for i in range(count)])
        reach *= 2
    return value, other


def round_plan(rows):
    tiles = -(-rows // LANES)
    groups = -(-tiles // SUB)
    sizes = [1, 1] if groups > 2 else []
    sizes += [2] * max(0, (groups - len(sizes) - 1) // 2)
    sizes += [1] * (groups - sum(sizes))
    plan, first = [], 0
    for size in sizes:
        plan.append((first, size, min(size * SUB, tiles - first * SUB)))
        first += size
    return plan


def turn(dist_ref, turned_ref):
    cells = dist_ref.shape[1]
    for s in range(SUB):
        for t in range(cells // LANES):
            block = dist_ref[s * LANES : (s + 1) * LANES, t * LANES : (t + 1) * LANES]
            turned_ref[pl.ds(t * LANES * SUB + s, LANES, stride=SUB), :] = block.T


def pick_rows(list_ref, row, turned_ref, picked_ref, out_ref, tiles):
    width = out_ref.shape[1]

    @pl.loop(0, width, unroll=8)
    def _(j):
        source = pl.ds(pl.multiple_of(list_ref[row, j] * SUB, SUB), SUB)
        picked_ref[pl.ds(pl.multiple_of(j * SUB, SUB), SUB), :] = turned_ref[source, :]

    for s in range(tiles):
        out_ref[s] = picked_ref[pl.ds(s, width, stride=SUB), :]


def first_send_kernel(
    place_ref, list_ref, dist_ref, normal_ref, volume_ref, cross_ref, ahead_ref, back_ref, least_ref,
    turned_ref, picked_ref,
):
    turn(dist_ref, turned_ref)
    for row, out_ref in ((2, ahead_ref), (3, back_ref), (1 - place_ref[1], cross_ref)):
        pick_rows(list_ref, row, turned_ref, picked_ref, out_ref, out_ref.shape[0])
    area = jnp.zeros_like(volume_ref)
    for k in range(FACES):
        part = [normal_ref[3 * k + a : 3 * k + a + 1, :] for a in range(3)]
        area = area + jnp.sqrt(part[0] * part[0] + part[1] * part[1] + part[2] * part[2])
    limit = volume_ref[...] / (HALF * math.sqrt(3.0) * area)
    least_ref[...] = jnp.broadcast_to(jnp.min(limit, axis=1, keepdims=True), least_ref.shape)


def turn_kernel(
    plan, place_ref, list_ref, dist_ref, after_ref, turned_ref, pair_ref, *refs,
):
    outs, picked_ref = refs[:-1], refs[-1]
    step = pl.program_id(0)
    turn(dist_ref, turned_ref.at[0])
    pick_rows(list_ref, place_ref[1], turned_ref.at[0], picked_ref, pair_ref, SUB)
    for i, (first, groups, tiles) in enumerate(plan):
        for g in range(groups):

            @pl.when(step == first + g)
            def _(i=i, g=g, tiles=tiles):
                here = min(SUB, tiles - g * SUB)
                for row, out_ref in zip((1 - place_ref[1], 2, 3), outs[3 * i : 3 * i + 3]):
                    pick_rows(list_ref, row, turned_ref.at[0], picked_ref, out_ref, here)


def rows8(row):
    return jnp.broadcast_to(row, (SUB, row.shape[-1]))


def last_speeds():
    index = lax.broadcasted_iota(jnp.int32, (SUB, LANES), 0).astype(F32) - HALF
    return [index + float(j * SUB) for j in range(NODES // SUB)]


def z_sums(tiles, speeds, powers):
    sums, terms = [], list(tiles)
    for p in range(powers):
        if p:
            terms = [t * c for t, c in zip(terms, speeds)]
        sums.append(terms[0] + terms[1] + terms[2])
    return sums


def rest_of_moments(sums, first):
    energy = 0.5 * (first * first * sums[0, 0] + sums[0, 1 + 1] + sums[2, 0])
    return [sums[0, 0], first * sums[0, 0], sums[0, 1], sums[1, 0], energy]


def add_rows(acc_ref, values, lanes):
    for m, value in enumerate(values):
        acc_ref[m * SUB : (m + 1) * SUB, lanes] += value


def sum_rows(acc_ref, count):
    return [jnp.sum(acc_ref[m * SUB : (m + 1) * SUB, :], axis=0, keepdims=True) for m in range(count)]


FLUX_KEYS = ((0, 0), (0, 1), (0, 2), (1, 0), (2, 0))
DIST_KEYS = ((0, 0), (0, 1), (0, 2), (0, 3), (1, 0), (1, 1), (1, 2), (2, 0), (2, 1), (3, 0))


def grow(carry, keys, sums, second):
    powers = [None, second, second * second, second * second * second]
    return tuple(
        c + (sums[i] if j == 0 else sums[i] * powers[j]) for c, (i, j) in zip(carry, keys)
    )


def moment_kernel(place_ref, dist_ref, after_ref, dist_sum_ref, dist_acc):
    step = pl.program_id(0)
    cells = dist_ref.shape[1]

    @pl.when(step == 0)
    def _():
        dist_acc[...] = jnp.zeros_like(dist_acc)

    speeds = last_speeds()
    tiles = range(NODES // SUB)
    first = (place_ref[0] + step).astype(F32) - HALF
    for t in range(cells // LANES):
        lanes = slice(t * LANES, (t + 1) * LANES)

        def body(y, carry, lanes=lanes):
            second = y.astype(F32) - HALF
            rows = [pl.ds(pl.multiple_of(y * NODES + j * SUB, SUB), SUB) for j in tiles]
            own = [dist_ref[r, lanes] for r in rows]
            return grow(carry, DIST_KEYS, z_sums(own, speeds, 4), second)

        zero = jnp.zeros((SUB, LANES), F32)
        part = lax.fori_loop(0, NODES, body, (zero,) * len(DIST_KEYS), unroll=4)
        s = dict(zip(DIST_KEYS, part))
        square = first * first
        add_rows(
            dist_acc,
            rest_of_moments(s, first)
            + [
                square * s[0, 0], s[0, 2], s[2, 0],
                first * s[0, 1], first * s[1, 0], s[1, 1],
                first * (square * s[0, 0] + s[0, 2] + s[2, 0]),
                square * s[0, 1] + s[0, 3] + s[2, 1],
                square * s[1, 0] + s[1, 2] + s[3, 0],
            ],
            lanes,
        )

    @pl.when(step == pl.num_programs(0) - 1)
    def _():
        dist_sum_ref[...] = jnp.concatenate(
            sum_rows(dist_acc, 14) + [jnp.zeros((2, cells), F32)], axis=0
        )


def speeds_at(index):
    first = jnp.floor((index + 0.5) * (1.0 / PLANE))
    rest = index - PLANE * first
    second = jnp.floor((rest + 0.5) * (1.0 / NODES))
    return first - HALF, second - HALF, rest - NODES * second - HALF


def time_row(least_ref, cells):
    return CFL * jnp.concatenate([least_ref[0:1, :]] * (cells // LANES), axis=1)


def face_kernel(
    rows, start, groups, rounds, timed, moves, place_ref, index_ref, normal_ref, stream_ref, turned_ref,
    before_ref, *refs,
):
    pairs, refs = refs[:groups], refs[groups:]
    received = [refs[3 * i : 3 * i + 3] for i in range(len(rounds))]
    flux_out_ref, flux_sum_ref, table_ref, flux_ref, flux_acc, ratio_ref = refs[-6:]
    if timed:
        least_ref, dist_ref, volume_ref, earlier_ref = refs[3 * len(rounds) :][:4]
        ratio_ref[...] = rows8(time_row(least_ref, flux_out_ref.shape[1]) / volume_ref[...])

    if moves:

        @pl.when(pl.program_id(0) > 0)
        def _():
            @pl.loop(0, flux_out_ref.shape[0] // SUB, unroll=8)
            def _(i):
                here = pl.ds(pl.multiple_of(i * SUB, SUB), SUB)
                flux_out_ref[here, :] = dist_ref[here, :] - ratio_ref[...] * earlier_ref[here, :]

    @pl.when(pl.program_id(0) == 0)
    def _():
        face_flux(
            rows, start, groups, rounds, place_ref, index_ref, normal_ref, stream_ref, turned_ref,
            before_ref, pairs, received, dist_ref if timed else None,
            flux_out_ref, flux_sum_ref, table_ref, flux_ref, flux_acc, ratio_ref,
        )


def face_flux(
    rows, start, groups, rounds, place_ref, index_ref, normal_ref, stream_ref, turned_ref,
    before_ref, pairs, received, dist_ref,
    flux_out_ref, flux_sum_ref, table_ref, flux_ref, flux_acc, ratio_ref,
):
    cells, width = flux_out_ref.shape[1], pairs[0].shape[1]
    odd = place_ref[1]
    block = SUB * LANES
    place_of, tiles = [], 0
    for i, count in enumerate(rounds):
        for g in range(count):
            place_of.append((received[i], g, min(SUB, received[i][0].shape[0] - g * SUB)))
            tiles += place_of[-1][2]

    speeds = []
    for g in range(groups):
        table_ref[g, 0 : cells * SUB, :] = turned_ref[g]
        (cross_ref, ahead_ref, back_ref), h, count = place_of[g]
        sources = ((pairs[g], 0, 1 - odd), (cross_ref, h, odd), (ahead_ref, h, 2), (back_ref, h, 3))
        for block_ref, part, slot in sources:
            for s in range(count):
                base = (cells + slot * width) * SUB + s
                table_ref[g, pl.ds(base, width, stride=SUB), :] = block_ref[part * SUB + s]
        inflow = cells + 4 * width
        table_ref[g, inflow * SUB : (inflow + 1) * SUB, :] = stream_ref[g * SUB : (g + 1) * SUB, :]
        at = lax.broadcasted_iota(jnp.int32, (SUB, LANES), 0) * LANES
        at = at + lax.broadcasted_iota(jnp.int32, (SUB, LANES), 1)
        at = at + (place_ref[0] * PLANE + start + g * block)
        speeds.append(speeds_at(at.astype(F32)))

    @pl.loop(0, cells, unroll=4)
    def _(c):
        here = pl.ds(pl.multiple_of(c * SUB, SUB), SUB)
        acc, low, full = ([None] * groups for _ in range(3))
        for k in range(FACES):
            source = pl.ds(pl.multiple_of(index_ref[k, c], SUB), SUB)
            normal = [normal_ref[3 * k + a, c] for a in range(3)]
            for g in range(groups):
                speed = sum(speeds[g][a] * normal[a] for a in range(1, 3)) + speeds[g][0] * normal[0]
                inward = jnp.minimum(speed, 0.0)
                part = inward * table_ref[g, source, :]
                acc[g] = part if k == 0 else acc[g] + part
                low[g] = inward if k == 0 else low[g] + inward
                full[g] = speed if k == 0 else full[g] + speed
        for g in range(groups):
            flux_ref[g, here, :] = acc[g] + (full[g] - low[g]) * table_ref[g, here, :]

    flux_acc[...] = jnp.zeros_like(flux_acc)
    parts = [slice(t * LANES, (t + 1) * LANES) for t in range(cells // LANES)]
    for q in range(tiles):
        g, s = divmod(q, SUB)
        turned = [
            flux_ref[g, pl.ds(t * LANES * SUB + s, LANES, stride=SUB), :].T for t in range(len(parts))
        ]
        sums = [[None] * 5 for _ in parts]
        for r in range(LANES // SUB):
            row = q * LANES + r * SUB
            counted = start + row < rows
            index = lax.broadcasted_iota(jnp.int32, (SUB, LANES), 0) + (
                place_ref[0] * PLANE + start + row
            )
            c = speeds_at(index.astype(F32))
            square = 0.5 * (c[0] * c[0] + c[1] * c[1] + c[2] * c[2])
            for t, lanes in enumerate(parts):
                flux = turned[t][r * SUB : (r + 1) * SUB, :]
                here = slice(row, row + SUB), lanes
                flux_out_ref[here] = (
                    flux if dist_ref is None else dist_ref[here] - ratio_ref[:, lanes] * flux
                )
                if counted:
                    terms = [flux, c[0] * flux, c[1] * flux, c[2] * flux, square * flux]
                    sums[t] = [p if z is None else z + p for z, p in zip(sums[t], terms)]
        for t, lanes in enumerate(parts):
            if sums[t][0] is not None:
                add_rows(flux_acc, sums[t], lanes)
    flux_sum_ref[...] = before_ref[...] + jnp.concatenate(
        sum_rows(flux_acc, 5) + [jnp.zeros((3, cells), F32)], axis=0
    )


def hydrodynamic_variables(moments):
    density = moments[0]
    mean = [moments[1 + axis] / density for axis in range(3)]
    square = mean[0] ** 2 + mean[1] ** 2 + mean[2] ** 2
    return density, mean, (2.0 * moments[4] / density - square) / 3.0


def relax_kernel(
    planes, place_ref, least_ref, moved_ref, dist_sum_ref, other_dist_ref, flux_sum_ref,
    other_flux_ref, volume_ref, out_ref,
    x_ref, y_ref, z_ref, cell_ref,
):
    step = pl.program_id(0)
    cells = moved_ref.shape[1]

    @pl.when(step == 0)
    def _():
        time_step = time_row(least_ref, cells)
        ratio = time_step / volume_ref[...]
        sums = [dist_sum_ref[m : m + 1, :] + other_dist_ref[m : m + 1, :] for m in range(14)]
        flux = [flux_sum_ref[m : m + 1, :] + other_flux_ref[m : m + 1, :] for m in range(5)]
        density, mean, _ = hydrodynamic_variables(sums)
        xx, yy, zz, xy, xz, yz = sums[5:11]
        pairs = ((xx, xy, xz), (xy, yy, yz), (xz, yz, zz))
        square = mean[0] ** 2 + mean[1] ** 2 + mean[2] ** 2
        heat = []
        for a in range(3):
            cross = mean[0] * pairs[a][0] + mean[1] * pairs[a][1] + mean[2] * pairs[a][2]
            heat.append(
                0.5
                * (
                    sums[11 + a] - mean[a] * (2.0 * sums[4]) - 2.0 * cross
                    + 2.0 * mean[a] * square * density
                )
            )
        new = [sums[m] - ratio * flux[m] for m in range(5)]
        density, mean, temp = hydrodynamic_variables(new)
        relax_time = MU_REF * jnp.exp(OMEGA * jnp.log(temp)) / (density * temp)
        relax = time_step / relax_time
        keep = 1.0 / (1.0 + relax)
        root = lax.rsqrt(2.0 * math.pi * temp)
        front = relax * keep * density * root * root * root
        along = (1.0 - PRANDTL) / (5.0 * density * temp * temp)
        for m, row in enumerate((keep, mean[0], temp, heat[0] * along, front)):
            cell_ref[m * SUB : (m + 1) * SUB, :] = rows8(row)
        nodes = lax.broadcasted_iota(jnp.int32, (NODES, cells), 0).astype(F32) - HALF
        for a, ref in ((1, y_ref), (2, z_ref)):
            rel = nodes - mean[a]
            square = rel * rel / temp
            for i, table in enumerate((jnp.exp(-0.5 * square), square, rel * heat[a] * along)):
                if a == 2:
                    ref[i * NODES : (i + 1) * NODES, :] = table
                    continue
                for y in range(NODES):
                    ref[i, y] = rows8(table[y : y + 1, :])

    keep, mean, temp, heat, front = [
        cell_ref[m * SUB : (m + 1) * SUB, :] for m in range(5)
    ]
    for p in range(planes):
        rel = (place_ref[0] + step * planes + p).astype(F32) - HALF - mean
        square = rel * rel / temp
        x_ref[0] = front * jnp.exp(-0.5 * square)
        x_ref[1] = square - 5.0
        x_ref[2] = rel * heat

        for t in range(cells // LANES):
            lanes = slice(t * LANES, (t + 1) * LANES)
            from_x = [x_ref[i, :, lanes] for i in range(3)]
            tiles = range(NODES // SUB)
            from_z = [
                [z_ref[i * NODES + j * SUB : i * NODES + (j + 1) * SUB, lanes] for j in tiles]
                for i in range(3)
            ]
            share = cell_ref[0:SUB, lanes]

            @pl.loop(0, NODES, unroll=4)
            def _(y, p=p, lanes=lanes, from_x=from_x, from_z=from_z, share=share):
                peak = from_x[0] * y_ref[0, y, :, lanes]
                square = from_x[1] + y_ref[1, y, :, lanes]
                along = from_x[2] + y_ref[2, y, :, lanes]
                for j in range(NODES // SUB):
                    row = pl.ds(pl.multiple_of(p * PLANE + y * NODES + j * SUB, SUB), SUB)
                    moved = moved_ref[row, lanes] * share
                    shape = (along + from_z[2][j]) * (square + from_z[1][j]) + 1.0
                    out_ref[row, lanes] = moved + peak * from_z[0][j] * shape


def params():
    return pltpu.CompilerParams(
        vmem_limit_bytes=VMEM_LIMIT, dimension_semantics=("arbitrary",)
    )


def whole(*shape):
    return pl.BlockSpec(shape, lambda i: (0,) * len(shape))


def planes_from(first, width, planes=1):
    return pl.BlockSpec((planes * PLANE, width), lambda i: (first // planes + i, 0))


SMEM = pl.BlockSpec(memory_space=pltpu.SMEM)
ANY = pl.BlockSpec(memory_space=pl.ANY)
HBM = pl.BlockSpec(memory_space=pltpu.HBM)


def hint(amount):
    return pl.CostEstimate(flops=0, bytes_accessed=amount, transcendentals=0)


def gate_kernel(*refs):
    pass


def gated(blocks, after):
    blocks = list(blocks)
    return pl.pallas_call(
        gate_kernel,
        in_specs=[HBM] * (len(blocks) + len(after)),
        out_specs=[HBM] * len(blocks),
        out_shape=[jax.ShapeDtypeStruct(block.shape, block.dtype) for block in blocks],
        input_output_aliases={i: i for i in range(len(blocks))},
        cost_estimate=hint(0),
        name="gate",
    )(*blocks, *after)


def first_sends(place, lists, dist, normals, volume, tiles):
    cells, width = dist.shape[1], lists.shape[1]
    return pl.pallas_call(
        first_send_kernel,
        grid=(1,),
        in_specs=[
            SMEM, SMEM, pl.BlockSpec((SUB * LANES, cells), lambda i: (0, 0)),
            whole(3 * FACES, cells), whole(1, cells),
        ],
        out_specs=[whole(tiles, width, LANES)] * 3 + [whole(SUB, LANES)],
        out_shape=[jax.ShapeDtypeStruct((tiles, width, LANES), F32)] * 3
        + [jax.ShapeDtypeStruct((SUB, LANES), F32)],
        scratch_shapes=[pltpu.VMEM((cells * SUB, LANES), F32), pltpu.VMEM((width * SUB, LANES), F32)],
        compiler_params=params(),
        cost_estimate=hint(4096),
        name="first_sends",
    )(place, lists, dist, normals, volume)


def turned_cells(place, lists, dist, plan, after):
    (rows, cells), width = dist.shape, lists.shape[1]
    block = SUB * LANES
    rounds = -(-rows // block)

    def part_of(first, groups):
        return pl.BlockSpec(
            (SUB, width, LANES), lambda i: (jnp.clip(i - first, 0, groups - 1), 0, 0)
        )

    outs = [(part_of(first, groups), tiles) for first, groups, tiles in plan for _ in range(3)]
    return pl.pallas_call(
        functools.partial(turn_kernel, plan),
        grid=(rounds,),
        in_specs=[
            SMEM, SMEM, pl.BlockSpec((block, cells), lambda i: (i, 0)), ANY,
        ],
        out_specs=[
            pl.BlockSpec((1, cells * SUB, LANES), lambda i: (i, 0, 0)),
            pl.BlockSpec((SUB, width, LANES), lambda i: (i, 0, 0)),
        ]
        + [spec for spec, _ in outs],
        out_shape=[
            jax.ShapeDtypeStruct((rounds, cells * SUB, LANES), F32),
            jax.ShapeDtypeStruct((-(-rows // LANES), width, LANES), F32),
        ]
        + [jax.ShapeDtypeStruct((tiles, width, LANES), F32) for _, tiles in outs],
        scratch_shapes=[pltpu.VMEM((width * SUB, LANES), F32)],
        compiler_params=params(),
        cost_estimate=hint(4096),
        name="turned_cells",
    )(place, lists, dist, after)


def dist_moments(place, dist, after):
    rows, cells = dist.shape
    return pl.pallas_call(
        moment_kernel,
        grid=(rows // PLANE,),
        in_specs=[SMEM, planes_from(0, cells), ANY],
        out_specs=whole(16, cells),
        out_shape=jax.ShapeDtypeStruct((16, cells), F32),
        scratch_shapes=[pltpu.VMEM((14 * SUB, cells), F32)],
        compiler_params=params(),
        cost_estimate=hint(4096),
        name="dist_moments",
    )(place, dist, after)


def face_sums(
    shape, place, index, normals, stream, turned, before, flux, pair, arrived, parts, after,
    timed=(), earlier=False,
):
    (rows, cells), width = shape, pair.shape[1]
    first, counts = parts[0][0], [groups for _, groups, _ in parts]
    groups = sum(counts)
    block = SUB * LANES
    offset = first // groups
    extra = () if flux is None else (flux,)
    steps = 1 + (offset if earlier else 0)
    here = pl.BlockSpec(
        (groups * block, cells), lambda i: (jnp.where(i == 0, offset, i - 1) if steps > 1 else offset, 0)
    )
    done = pl.BlockSpec((groups * block, cells), lambda i: (jnp.maximum(i - 1, 0), 0))
    timed_specs = [whole(SUB, LANES), here, whole(1, cells), done if steps > 1 else ANY]
    received = [block for group in arrived for block in group]
    if timed and not extra:
        aliases, extra = {}, (timed[1],)
    else:
        aliases = {6 + groups + len(received) + len(timed): 0} if extra else {}
    return pl.pallas_call(
        functools.partial(face_kernel, rows, first * block, groups, counts, bool(timed), steps > 1),
        grid=(steps,),
        in_specs=[
            SMEM, SMEM, SMEM,
            pl.BlockSpec((groups * SUB, LANES), lambda _: (offset, 0)),
            pl.BlockSpec((groups, cells * SUB, LANES), lambda _: (offset, 0, 0)),
            whole(8, cells),
        ]
        + [
            pl.BlockSpec((SUB, width, LANES), lambda _, g=g: (first + g, 0, 0))
            for g in range(groups)
        ]
        + [whole(*block.shape) for block in received]
        + (timed_specs if timed else [ANY] * len(extra))
        + [ANY] * len(after),
        out_specs=[here, whole(8, cells)],
        out_shape=[
            jax.ShapeDtypeStruct((rows, cells), F32),
            jax.ShapeDtypeStruct((8, cells), F32),
        ],
        scratch_shapes=[
            pltpu.VMEM((groups, (cells + 4 * width + 1) * SUB, LANES), F32),
            pltpu.VMEM((groups, cells * SUB, LANES), F32),
            pltpu.VMEM((5 * SUB, cells), F32),
            pltpu.VMEM((SUB, cells), F32),
        ],
        input_output_aliases=aliases,
        compiler_params=params(),
        cost_estimate=hint(4096),
        name="face_sums",
    )(
        place, index, normals, stream, turned, before,
        *([pair] * groups), *received, *timed, *extra, *after,
    )


def step_planes(planes):
    return 2 - planes % 2


def relaxed(place, least, moved, dist_sums, flux_sums, volume):
    rows, cells = moved.shape
    planes = step_planes(rows // PLANE)
    return pl.pallas_call(
        functools.partial(relax_kernel, planes),
        grid=(rows // PLANE // planes,),
        in_specs=[
            SMEM, whole(SUB, LANES), planes_from(0, cells, planes), whole(16, cells),
            whole(16, cells), whole(8, cells), whole(8, cells), whole(1, cells),
        ],
        out_specs=planes_from(0, cells, planes),
        out_shape=jax.ShapeDtypeStruct((rows, cells), F32),
        scratch_shapes=[
            pltpu.VMEM((3, SUB, cells), F32),
            pltpu.VMEM((3, NODES, SUB, cells), F32),
            pltpu.VMEM((3 * NODES, cells), F32),
            pltpu.VMEM((5 * SUB, cells), F32),
        ],
        compiler_params=params(),
        cost_estimate=pl.CostEstimate(
            flops=10 * rows * cells, bytes_accessed=8 * rows * cells, transcendentals=0
        ),
        name="relaxed",
    )(place, least, moved, *dist_sums, *flux_sums, volume)


def local(dist, free_stream, area_normal, cell_volume, face_nbr, face_type, send_list):
    rows, cells = dist.shape
    planes = rows // PLANE
    dirs, width = send_list.shape
    block = SUB * LANES
    rounds = -(-rows // block)
    place = jnp.stack([lax.axis_index("vel") * planes, lax.axis_index("space") % 2]).astype(jnp.int32)

    def sent(blocks):
        return (
            swapped(blocks[0], "space", 1),
            passed_along(blocks[1], "space", neighbour_steps[2]),
            passed_along(blocks[2], "space", neighbour_steps[3]),
        )

    plan = round_plan(rows)
    volume = cell_volume.reshape(1, cells)
    own = jnp.arange(cells, dtype=jnp.int32)[None, :]
    inflow = cells + dirs * width
    index = jnp.where(face_type == 0, face_nbr, jnp.where(face_type == 1, inflow, own)) * SUB
    stream = jnp.pad(free_stream, (0, rounds * block - rows)).reshape(rounds * SUB, LANES)

    shift, n_space = 1, lax.axis_size("space")
    *blocks, least = first_sends(place, send_list, dist, area_normal, volume, plan[0][2])
    turned, pair, *later = turned_cells(place, send_list, dist, plan[1:], blocks[0])
    arrived, pending, gate_after = [], [], []
    flux, flux_sum, dist_sum, moved = None, jnp.zeros((8, cells), F32), None, False
    for i, part in enumerate(plan):
        arrived.append(sent(blocks))
        least_now, least_known = least, shift >= n_space
        for _ in range(2 if i == 2 else 1):
            if shift < n_space:
                least = jnp.minimum(least, passed_along(least, "space", shift))
                shift *= 2
        if i == 0:
            gate_after = []
        elif i == 1:
            pair = swapped(pair, "space", 0)
            dist_sum = dist_moments(place, dist, blocks[0])
            gate_after = [dist_sum, pair]
        else:
            parts = plan[0:2] if i == 2 else plan[i - 1 : i]
            timed = (least_now, dist, volume) if least_known else ()
            flux, flux_sum = face_sums(
                dist.shape, place, index, area_normal, stream, turned, flux_sum, flux,
                pair, arrived[0:2] if i == 2 else arrived[i - 1 : i], parts, [blocks[0]],
                timed, bool(timed) and not moved,
            )
            moved = bool(timed)
            gate_after = [flux_sum]
        if i == 2:
            dist_sum = halves_over(dist_sum, "vel")
            gate_after += dist_sum
        if i + 1 < len(plan):
            blocks = later[3 * i : 3 * i + 3]
            rest = [least, pair] if i == 0 else [least]
            gated_arrays = gated([*blocks, *rest], [*arrived[-1], *gate_after])
            blocks, least = gated_arrays[:3], gated_arrays[3]
            if i == 0:
                pair = gated_arrays[4]
    if len(plan) == 1:
        dist_sum = dist_moments(place, dist, blocks[0])
        pair = swapped(pair, "space", 0)
    if len(plan) < 3:
        dist_sum = halves_over(dist_sum, "vel")
    while shift < n_space:
        least = jnp.minimum(least, passed_along(least, "space", shift))
        shift *= 2
    done = 0 if len(plan) < 3 else len(plan) - 1
    flux, flux_sum = face_sums(
        dist.shape, place, index, area_normal, stream, turned, flux_sum, flux,
        pair, arrived[done:], plan[done:], [], (least, dist, volume), done > 0 and not moved,
    )
    return relaxed(place, least, flux, dist_sum, halves_over(flux_sum, "vel"), volume)


def solution(mesh):
    return jax.shard_map(
        local,
        mesh=mesh,
        in_specs=(
            P("vel", "space"),
            P("vel"),
            P(None, "space"),
            P("space"),
            P(None, "space"),
            P(None, "space"),
            P(None, "space"),
        ),
        out_specs=P("vel", "space"),
        check_vma=False,
    )
```
